32 devices in a mesh: sec: 2 (over core), grp: 4 (over y, x), blk: 4 (over z).
Axes of the slice: x: 2, y: 2, z: 4, core: 2. Of those that a mesh axis runs over, the one named last changes fastest.
Arguments:
- atm_flux: bfloat16 [2, 60, 65536], P(None, None, ('sec', 'grp', 'blk')), may hold values from -25 to 25
- tile_bank: bfloat16 [128, 128, 128], replicated, may hold values from -1 to 1
- pair_count: int32 [32], P(('sec', 'grp', 'blk')), may hold values from 32 to 128, as said below
- pair_source: int32 [4096], P(('sec', 'grp', 'blk')), may hold values from 0 to 15
- pair_tile: int32 [4096], P(('sec', 'grp', 'blk')), may hold values from 0 to 127
- pair_target: int32 [4096], P(('sec', 'grp', 'blk')), may hold values from 0 to 7
- tracers: bfloat16 [32, 60, 8192], P(None, None, ('sec', 'grp', 'blk')), may hold values from -6 to 6
- diffusivity: float32 [31, 8192], P(None, ('sec', 'grp', 'blk')), may hold values from 0.2 to 5
- column_depth: int32 [8192], P(('sec', 'grp', 'blk')), may hold values from 0 to 32
Outputs:
- mixed_tracers: float32 [32, 60, 8192], P(None, None, ('sec', 'grp', 'blk'))
The draws below stay inside these ranges and needn't reach their ends.
Inputs may be any that keep to these rules, and one draw needn't show every extreme that they name: `pair_count`: pairs at positions 127 and below that are at or past a device's count are unused; some device has exactly 128 live pairs. `pair_target`: a target t names ocean block t % 2 of the device at blk index t // 2 with the same sec and grp. Levels at index column_depth and below are dry; 0 marks a land column.
All inputs are finite; a program needn't handle non-finite values.
Results may differ from the reference program's by a relative error of at most 0.013.
Values may be sent and summed in bfloat16 or wider, within the bound.
A program may use at most 64 MiB of HBM per device.

```python
import math
import jax
import jax.numpy as jnp
from jax import lax

FIELDS = 60
TILE = 128
SUB = 2
SRC_BLOCKS = 16
PAIRS = 128
OCN_BLOCKS = 2
LEVELS = 32
BANK = 128
DEVICE_COUNT = 32
ATM_ROWS = 65536
NCOL = 8192
TARGETS = 8
N_BLK = 4


def draw_atm_flux(key, part):
    rough_key, mean_key = jax.random.split(jax.random.fold_in(key, 11))
    position = jnp.arange(ATM_ROWS, dtype=jnp.float32) / ATM_ROWS
    rising = 1.0 + 2.0 * position
    rough_part = jnp.clip(jax.random.normal(rough_key, (SUB, FIELDS, ATM_ROWS), jnp.float32), -4.0, 4.0)
    field_mean = jax.random.uniform(mean_key, (SUB, FIELDS, 1), jnp.float32, 0.2, 0.6)
    return (rising[None, None, :] * (field_mean + rough_part)).astype(jnp.bfloat16)


def draw_tile_bank(key, part):
    spread = (PAIRS * TILE / 8.0) ** (-0.5)
    offset_mean = 4.0 / (PAIRS * TILE)
    tile_key = jax.random.fold_in(key, 23)
    rough_part = jnp.clip(jax.random.normal(tile_key, (BANK, TILE, TILE), jnp.float32), -4.0, 4.0)
    return (rough_part * spread + offset_mean).astype(jnp.bfloat16)


def draw_pair_count(key, part):
    first_key, second_key, full_key = jax.random.split(jax.random.fold_in(key, 37), 3)
    first_draw = jax.random.randint(first_key, (DEVICE_COUNT,), 0, PAIRS)
    second_draw = jax.random.randint(second_key, (DEVICE_COUNT,), 0, PAIRS)
    counts = PAIRS // 4 + 3 * first_draw * second_draw // (4 * PAIRS)
    full_device = jax.random.randint(full_key, (), 0, DEVICE_COUNT)
    light_device = (full_device + 1) % DEVICE_COUNT
    device_ids = jnp.arange(DEVICE_COUNT, dtype=jnp.int32)
    counts = jnp.where(device_ids == light_device, PAIRS // 4, counts)
    return jnp.where(device_ids == full_device, PAIRS, counts).astype(jnp.int32)


def place_ends(values, key, low, largest):
    dims = values.shape
    index_at = [jax.random.randint(jax.random.fold_in(key, axis), (), 0, dims[axis]) for axis in range(len(dims))]
    values = values.at[tuple(index_at)].set(low)
    longest = dims.index(max(dims))
    index_at[longest] = (index_at[longest] + 1) % dims[longest]
    return values.at[tuple(index_at)].set(largest)


def levels(rng, extent, shards, least, largest):
    level = 1.0
    for axis_at, blocks in shards:
        draws = jax.random.uniform(jax.random.fold_in(jax.random.fold_in(rng, 6), axis_at), (blocks,), jnp.float32, least / len(shards), largest / len(shards))
        level = level * jnp.repeat(jnp.exp(draws), extent[axis_at] // blocks).reshape((-1,) + (1,) * (len(extent) - 1 - axis_at))
    return level


def normal_values(stream_key, dims, scale, most, shards=(), held_as=jnp.bfloat16):
    values = jax.random.normal(stream_key, dims, jnp.float32) * scale
    if len(shards) > 0:
        values = levels(stream_key, dims, shards, -0.22, 0.18) * values
    return jnp.clip(values, min=-most, max=most).astype(held_as)


def setup_inputs(seed: int = 0) -> dict:
    streams_of = jax.random.split(jax.random.key(seed), 10)
    atm_flux = draw_atm_flux(jax.random.fold_in(streams_of[9], 71), 0)
    tile_bank = draw_tile_bank(jax.random.fold_in(streams_of[9], 71), 0)
    pair_count = draw_pair_count(jax.random.fold_in(streams_of[9], 71), 0)
    pair_source = place_ends(jax.random.randint(streams_of[3], (DEVICE_COUNT * PAIRS,), 0, SRC_BLOCKS), jax.random.fold_in(streams_of[3], 1), 0, SRC_BLOCKS - 1).astype(jnp.int32)
    pair_tile = place_ends(jax.random.randint(streams_of[4], (DEVICE_COUNT * PAIRS,), 0, BANK), jax.random.fold_in(streams_of[4], 1), 0, BANK - 1).astype(jnp.int32)
    pair_target = place_ends(jax.random.randint(streams_of[5], (DEVICE_COUNT * PAIRS,), 0, TARGETS), jax.random.fold_in(streams_of[5], 1), 0, TARGETS - 1).astype(jnp.int32)
    tracers = normal_values(streams_of[6], (LEVELS, FIELDS, NCOL), 1.0, 6.0, ((2, 32),))
    diffusivity = jnp.clip(jnp.exp(math.log(5.0) - 3.218876 * jax.random.uniform(streams_of[7], (LEVELS - 1, NCOL), jnp.float32) ** levels(streams_of[7], (LEVELS - 1, NCOL), ((1, 32),), -0.2, 0.2)), 0.2, 5.0)
    column_depth = place_ends(jax.random.randint(streams_of[8], (NCOL,), 0, LEVELS + 1), jax.random.fold_in(streams_of[8], 1), 0, LEVELS).astype(jnp.int32)
    return dict(atm_flux=atm_flux, tile_bank=tile_bank, pair_count=pair_count, pair_source=pair_source, pair_tile=pair_tile, pair_target=pair_target, tracers=tracers, diffusivity=diffusivity, column_depth=column_depth)


def column_factors(diffusivity, column_depth):
    layer_count = diffusivity.shape[0] + 1
    layer_ids = jnp.arange(layer_count, dtype=jnp.int32)
    active = layer_ids[:, None] < column_depth[None, :]
    interior = diffusivity * active[1:].astype(diffusivity.dtype)
    boundary = jnp.zeros_like(diffusivity[:1])
    coupling = jnp.concatenate([boundary, interior, boundary], axis=0)
    diagonal = 1.0 + coupling[:-1] + coupling[1:]
    inverse_pivot = []
    upper_ratio = []
    for k in range(layer_count):
        if k == 0:
            pivot_entry = diagonal[0]
        else:
            pivot_entry = diagonal[k] + coupling[k] * upper_ratio[k - 1]
        inverse = 1.0 / pivot_entry
        inverse_pivot.append(inverse)
        upper_ratio.append(-coupling[k + 1] * inverse)
    live_mask = active.astype(diffusivity.dtype)[:, None, :]
    surface = (column_depth > 0).astype(diffusivity.dtype)
    return coupling, inverse_pivot, upper_ratio, live_mask, surface


def mix_once(column_state, surface_term, factors):
    coupling, inverse_pivot, upper_ratio, live_mask, surface = factors
    right_side = column_state.at[0].add(surface_term * surface[None, :]) * live_mask
    forward = []
    for k in range(right_side.shape[0]):
        if k == 0:
            carried = right_side[0]
        else:
            carried = right_side[k] + coupling[k][None, :] * forward[k - 1]
        forward.append(carried * inverse_pivot[k][None, :])
    solved = [forward[-1]]
    for k in range(right_side.shape[0] - 2, -1, -1):
        solved.append(forward[k] - upper_ratio[k][None, :] * solved[-1])
    return jnp.stack(solved[::-1])


def remap_device(flux_blocks, live_count, sources, tile_ids, targets, tile_bank):
    picked = jnp.take(flux_blocks, sources, axis=1).astype(jnp.float32)
    chosen = jnp.take(tile_bank, tile_ids, axis=0).astype(jnp.float32)
    products = jnp.einsum("spr,prc->psc", picked, chosen)
    live_pairs = (jnp.arange(PAIRS, dtype=jnp.int32) < live_count).astype(jnp.float32)
    products = products * live_pairs[:, None, None]
    zero_sums = jnp.zeros((N_BLK, SUB * FIELDS, OCN_BLOCKS, TILE), jnp.float32)
    summed = zero_sums.at[targets // OCN_BLOCKS, :, targets % OCN_BLOCKS].add(products)
    return summed.astype(jnp.bfloat16)


def reference(atm_flux, tile_bank, pair_count, pair_source, pair_tile, pair_target, tracers, diffusivity, column_depth):
    stacked = SUB * FIELDS
    group_count = DEVICE_COUNT // N_BLK
    blocks = atm_flux.reshape(stacked, DEVICE_COUNT, SRC_BLOCKS, TILE).transpose(1, 0, 2, 3)
    blocks = blocks.reshape(group_count, N_BLK, stacked, SRC_BLOCKS, TILE)

    def shaped(a):
        return a.reshape(group_count, N_BLK, PAIRS)

    def one_group(group_args):
        flux_group, counts, sources, tile_ids, targets = group_args

        def one_device(device_args):
            return remap_device(*device_args, tile_bank)

        outgoing = lax.map(one_device, (flux_group, counts, sources, tile_ids, targets))
        received = jnp.sum(outgoing.astype(jnp.float32), axis=0)
        ocean_part = jnp.sum(received, axis=(0, 2, 3))
        atm_part = jnp.sum(flux_group.astype(jnp.float32), axis=(0, 2, 3))
        return received, atm_part, ocean_part

    received, atm_parts, ocean_parts = lax.map(
        one_group,
        (blocks, pair_count.reshape(group_count, N_BLK), shaped(pair_source), shaped(pair_tile), shaped(pair_target)))
    device_width = OCN_BLOCKS * TILE
    forcing_all = received.reshape(DEVICE_COUNT, SUB, FIELDS, device_width)
    atm_total = jnp.sum(atm_parts, axis=0).reshape(SUB, FIELDS)
    ocean_total = jnp.sum(ocean_parts, axis=0).reshape(SUB, FIELDS)
    correction = (atm_total * (OCN_BLOCKS / SRC_BLOCKS) - ocean_total) / NCOL

    def mix_device(device_index, result):
        first_column = jnp.asarray(device_index * device_width).astype(jnp.int32)
        column_state = lax.dynamic_slice_in_dim(tracers, first_column, device_width, 2).astype(jnp.float32)
        factors = column_factors(
            lax.dynamic_slice_in_dim(diffusivity, first_column, device_width, 1),
            lax.dynamic_slice_in_dim(column_depth, first_column, device_width, 0))
        for substep in range(SUB):
            column_state = mix_once(column_state, forcing_all[device_index, substep] + correction[substep][:, None], factors)
        return lax.dynamic_update_slice_in_dim(result, column_state, first_column, 2)

    return lax.fori_loop(0, DEVICE_COUNT, mix_device, jnp.zeros((LEVELS, FIELDS, NCOL), jnp.float32))
```

```python
import functools

import jax
import jax.numpy as jnp
from jax import lax
from jax.experimental import pallas as pl
from jax.experimental.pallas import tpu as pltpu
from jax.sharding import PartitionSpec as P

MESH = pl.DeviceIdType.MESH


def up(value, unit):
    return -(-value // unit) * unit


def couple_kernel(
    blk_count,
    grp_count,
    side_count,
    ocean_blocks,
    scale,
    inverse_columns,
    count_ref,
    source_ref,
    tile_ref,
    target_ref,
    diffusivity_ref,
    depth_ref,
    flux_hbm,
    bank_hbm,
    tracers_hbm,
    mixed_hbm,
    response_ref,
    forced_ref,
    flux,
    bank,
    tracers,
    state,
    blocks,
    running,
    lists,
    lists_smem,
    outgoing,
    arrived,
    own_total,
    line_totals,
    line_sum,
    side_totals,
    couple,
    weight,
    carry,
    ratio,
    local_sem,
    send_sem,
    recv_sem,
    line_send,
    line_recv,
    side_send,
    side_recv,
):
    sec, grp, blk = lax.axis_index("sec"), lax.axis_index("grp"), lax.axis_index("blk")
    side = sec * grp_count + grp

    def line_peer(step):
        return lax.rem(blk + step, blk_count)

    def side_peer(step):
        return lax.rem(side + step, side_count)

    def line_id(peer):
        return (sec, grp, peer)

    def side_id(peer):
        return (peer // grp_count, lax.rem(peer, grp_count), blk)

    flux_copy = pltpu.make_async_copy(flux_hbm, flux, local_sem.at[0])
    bank_copy = pltpu.make_async_copy(bank_hbm, bank, local_sem.at[1])
    tracers_copy = pltpu.make_async_copy(tracers_hbm, tracers, local_sem.at[2])
    flux_copy.start()
    bank_copy.start()
    tracers_copy.start()

    barrier = pltpu.get_barrier_semaphore()

    @pl.loop(1, blk_count)
    def _(step):
        pl.semaphore_signal(barrier, inc=1, device_id=line_id(line_peer(step)), device_id_type=MESH)

    @pl.loop(1, side_count)
    def _(step):
        pl.semaphore_signal(barrier, inc=1, device_id=side_id(side_peer(step)), device_id_type=MESH)

    pairs = source_ref.shape[1]
    slots = lists.shape[1]
    live_count = count_ref[0]
    square = (pairs, pairs)
    row_at = lax.broadcasted_iota(jnp.int32, square, 0)
    lane_at = lax.broadcasted_iota(jnp.int32, square, 1)
    target_row = jnp.broadcast_to(target_ref[...], square)
    target_col = jnp.transpose(target_row)
    source_col = jnp.transpose(jnp.broadcast_to(source_ref[...], square))
    tile_col = jnp.transpose(jnp.broadcast_to(tile_ref[...], square))
    live_row = lane_at < live_count
    live_col = row_at < live_count
    hits = jnp.where((target_col == lane_at) & live_col, 1, 0)
    counts = jnp.sum(hits, axis=0, keepdims=True)
    padded = jnp.broadcast_to(lax.div(counts + 1, 2) * 2, square)
    before = jnp.where(lane_at < target_col, padded, 0)
    rank = jnp.where((target_row == target_col) & (lane_at < row_at) & live_row, 1, 0)
    slot = jnp.sum(before + rank, axis=1, keepdims=True)
    slot = jnp.where(live_col, jnp.broadcast_to(slot, square), slots)
    block_count = blocks.shape[0] - 1
    steps = running.shape[0] - 1
    lists[...] = jnp.zeros(lists.shape, jnp.int32)
    for first in range(0, slots, pairs):
        lanes = slice(first, first + pairs)
        chosen = slot == lane_at + first
        sources = jnp.sum(jnp.where(chosen, source_col - block_count, 0), axis=0, keepdims=True)
        tiles = jnp.sum(jnp.where(chosen, tile_col, 0), axis=0, keepdims=True)
        targets = jnp.sum(jnp.where(chosen, target_col + 1, 0), axis=0, keepdims=True)
        lists[0:1, lanes] = jnp.clip(sources + block_count, 0, block_count)
        lists[1:2, lanes] = jnp.clip(tiles, 0, bank.shape[0] - 1)
        lists[2:3, lanes] = targets
    upto = jnp.where(row_at <= lane_at, jnp.transpose(padded), 0)
    ends = lax.div(jnp.sum(upto, axis=0, keepdims=True), 2) - 1
    lists[8:9, 0:pairs] = jnp.where(counts > 0, jnp.clip(ends, 0, steps), steps)
    lists_copy = pltpu.make_async_copy(lists, lists_smem, local_sem.at[3])
    lists_copy.start()

    levels, columns = tracers.shape[0], tracers.shape[2]
    depth = depth_ref[...]
    level_at = lax.broadcasted_iota(jnp.int32, (levels, columns), 0)
    wet = jnp.where(level_at < depth, 1.0, 0.0)
    couple[0:1, :] = jnp.zeros((1, columns), jnp.float32)
    couple[1:levels, :] = diffusivity_ref[...] * wet[1:levels]
    couple[levels : levels + 1, :] = jnp.zeros((1, columns), jnp.float32)
    previous = jnp.zeros((1, columns), jnp.float32)
    forward = []
    for k in range(levels):
        a = couple[k : k + 1, :]
        b = couple[k + 1 : k + 2, :]
        inverse = 1.0 / (1.0 + a + b - a * previous)
        previous = b * inverse
        weight[k : k + 1, :] = jnp.where(depth > k, inverse, 0.0)
        carry[k : k + 1, :] = a * inverse
        ratio[k : k + 1, :] = previous
    for sweep in range(2):
        right = response_ref.at[0]
        unit = jnp.zeros((1, columns), jnp.float32)
        forward = []
        for k in range(levels):
            if sweep == 0:
                given = weight[0:1, :] if k == 0 else jnp.zeros((1, columns), jnp.float32)
            else:
                given = right[k : k + 1, :] * weight[k : k + 1, :]
            unit = given + carry[k : k + 1, :] * unit
            forward.append(unit)
        solved = forward[-1]
        response_ref[sweep, levels - 1 : levels, :] = solved
        for k in range(levels - 2, -1, -1):
            solved = forward[k] + ratio[k : k + 1, :] * solved
            response_ref[sweep, k : k + 1, :] = solved

    flux_copy.wait()
    subs, fields = flux.shape[0], flux.shape[1]
    width = blocks.shape[2]
    half = blocks.shape[1] // subs
    rows = blocks.shape[1]
    blocks[...] = jnp.zeros(blocks.shape, blocks.dtype)
    for b in range(block_count):
        for s in range(subs):
            blocks[b, s * half : s * half + fields, :] = flux[s, :, b * width : (b + 1) * width]
    running[steps] = jnp.zeros((rows, width), jnp.float32)
    spread = jnp.zeros((rows, width), jnp.float32)
    for b in range(block_count):
        spread = spread + blocks[b].astype(jnp.float32)
    own_total[...] = spread * scale

    lists_copy.wait()
    bank_copy.wait()

    def add_step(step, held):
        total, last = held
        first, second = 2 * step, 2 * step + 1
        target = lists_smem[2, first]
        left = jnp.concatenate([blocks[lists_smem[0, first]], blocks[lists_smem[0, second]]], axis=1)
        right = jnp.concatenate([bank[lists_smem[1, first]], bank[lists_smem[1, second]]], axis=0)
        keep = jnp.where(target == last, 1.0, 0.0).astype(jnp.float32)
        total = total * keep + jnp.dot(left, right, preferred_element_type=jnp.float32)
        running[step] = total
        return total, target

    lax.fori_loop(
        0, steps, add_step, (jnp.zeros((rows, width), jnp.float32), jnp.int32(-1)), unroll=4
    )

    @pl.loop(0, blk_count)
    def _(peer):
        spread = own_total[...]
        for o in range(ocean_blocks):
            out = running[lists_smem[8, peer * ocean_blocks + o]].astype(jnp.bfloat16)
            outgoing[peer, :, o * width : (o + 1) * width] = out
            spread = spread - out.astype(jnp.float32)
        own_total[...] = spread

    total_row = jnp.sum(jnp.transpose(own_total[...]), axis=0, keepdims=True)
    line_totals[blk] = jnp.broadcast_to(total_row, (8, rows))

    pl.semaphore_wait(barrier, blk_count - 1 + side_count - 1)

    def line_copy(peer, slot_at):
        return pltpu.make_async_remote_copy(
            src_ref=line_totals.at[blk],
            dst_ref=line_totals.at[slot_at],
            send_sem=line_send.at[peer],
            recv_sem=line_recv.at[slot_at],
            device_id=line_id(peer),
            device_id_type=MESH,
        )

    def data_copy(peer, slot_at):
        return pltpu.make_async_remote_copy(
            src_ref=outgoing.at[peer],
            dst_ref=arrived.at[slot_at],
            send_sem=send_sem.at[peer],
            recv_sem=recv_sem.at[slot_at],
            device_id=line_id(peer),
            device_id_type=MESH,
        )

    def side_copy(peer, slot_at):
        return pltpu.make_async_remote_copy(
            src_ref=line_sum,
            dst_ref=side_totals.at[slot_at],
            send_sem=side_send.at[peer],
            recv_sem=side_recv.at[slot_at],
            device_id=side_id(peer),
            device_id_type=MESH,
        )

    @pl.loop(1, blk_count)
    def _(step):
        line_copy(line_peer(step), blk).start()

    @pl.loop(1, blk_count)
    def _(step):
        data_copy(line_peer(step), blk).start()

    tracers_copy.wait()

    def forward_level(source):
        def level(k, held):
            held = source[k].astype(jnp.float32) * weight[pl.ds(k, 1), :] + carry[pl.ds(k, 1), :] * held
            state[k] = held
            return held

        return level

    def back_level(i, held):
        k = levels - 2 - i
        held = state[k] + ratio[pl.ds(k, 1), :] * held
        state[k] = held
        return held

    nothing = jnp.zeros((fields, columns), jnp.float32)
    bottom = lax.fori_loop(0, levels, forward_level(tracers), nothing)

    @pl.loop(1, blk_count)
    def _(step):
        peer = line_peer(step)
        line_copy(peer, peer).wait_recv()

    summed = line_totals[0]
    for p in range(1, blk_count):
        summed = summed + line_totals[p]
    line_sum[...] = summed

    @pl.loop(1, side_count)
    def _(step):
        side_copy(side_peer(step), side).start()

    lax.fori_loop(0, levels - 1, back_level, bottom)
    bottom = lax.fori_loop(0, levels, forward_level(state), nothing)
    lax.fori_loop(0, levels - 1, back_level, bottom)
    mixed_copy = pltpu.make_async_copy(state, mixed_hbm, local_sem.at[4])
    mixed_copy.start()

    @pl.loop(1, side_count)
    def _(step):
        peer = side_peer(step)
        side_copy(peer, peer).wait_recv()

    side_totals[side] = line_sum[...]
    everything = side_totals[0]
    for p in range(1, side_count):
        everything = everything + side_totals[p]
    correction = jnp.transpose(jnp.broadcast_to(everything[0:1, :] * inverse_columns, (rows, rows)))

    @pl.loop(1, blk_count)
    def _(step):
        peer = line_peer(step)
        data_copy(peer, peer).wait_recv()

    arrived[blk] = outgoing[blk]
    for o in range(ocean_blocks):
        lanes = slice(o * width, (o + 1) * width)
        forced = arrived[0, :, lanes].astype(jnp.float32)
        for p in range(1, blk_count):
            forced = forced + arrived[p, :, lanes].astype(jnp.float32)
        forced_ref[:, lanes] = forced + correction

    mixed_copy.wait()

    @pl.loop(1, blk_count)
    def _(step):
        peer = line_peer(step)
        line_copy(peer, blk).wait_send()
        data_copy(peer, blk).wait_send()

    @pl.loop(1, side_count)
    def _(step):
        side_copy(side_peer(step), side).wait_send()


def body(
    atm_flux,
    tile_bank,
    pair_count,
    pair_source,
    pair_tile,
    pair_target,
    tracers,
    diffusivity,
    column_depth,
):
    subs, fields, atm_rows = atm_flux.shape
    width = tile_bank.shape[1]
    block_count = atm_rows // width
    levels, _, columns = tracers.shape
    ocean_blocks = columns // width
    blk_count, grp_count = lax.axis_size("blk"), lax.axis_size("grp")
    side_count = lax.axis_size("sec") * grp_count
    pairs = pair_source.shape[0]
    half = up(fields, 64)
    rows = subs * half
    slot_count = up(pairs + blk_count * ocean_blocks, 2)
    steps = slot_count // 2
    steps_up = up(steps, 4)
    slots = up(2 * steps_up, 128)
    f32, bf16 = jnp.float32, jnp.bfloat16
    vmem = pl.BlockSpec(memory_space=pltpu.VMEM)
    smem = pl.BlockSpec(memory_space=pltpu.SMEM)
    anywhere = pl.BlockSpec(memory_space=pl.ANY)
    mixed, response, forced = pl.pallas_call(
        functools.partial(
            couple_kernel,
            blk_count,
            grp_count,
            side_count,
            ocean_blocks,
            ocean_blocks / block_count,
            1.0 / (columns * blk_count * side_count),
        ),
        out_shape=(
            jax.ShapeDtypeStruct((levels, fields, columns), f32),
            jax.ShapeDtypeStruct((2, levels, columns), f32),
            jax.ShapeDtypeStruct((rows, columns), f32),
        ),
        in_specs=[smem, vmem, vmem, vmem, vmem, vmem, anywhere, anywhere, anywhere],
        out_specs=(anywhere, vmem, vmem),
        scratch_shapes=[
            pltpu.VMEM(atm_flux.shape, bf16),
            pltpu.VMEM(tile_bank.shape, bf16),
            pltpu.VMEM(tracers.shape, bf16),
            pltpu.VMEM(tracers.shape, f32),
            pltpu.VMEM((block_count + 1, rows, width), bf16),
            pltpu.VMEM((steps_up + 1, rows, width), f32),
            pltpu.VMEM((16, slots), jnp.int32),
            pltpu.SMEM((16, slots), jnp.int32),
            pltpu.VMEM((blk_count, rows, columns), bf16),
            pltpu.VMEM((blk_count, rows, columns), bf16),
            pltpu.VMEM((rows, width), f32),
            pltpu.VMEM((blk_count, 8, rows), f32),
            pltpu.VMEM((8, rows), f32),
            pltpu.VMEM((side_count, 8, rows), f32),
            pltpu.VMEM((levels + 8, columns), f32),
            pltpu.VMEM((levels, columns), f32),
            pltpu.VMEM((levels, columns), f32),
            pltpu.VMEM((levels, columns), f32),
            pltpu.SemaphoreType.DMA((5,)),
            pltpu.SemaphoreType.DMA((blk_count,)),
            pltpu.SemaphoreType.DMA((blk_count,)),
            pltpu.SemaphoreType.DMA((blk_count,)),
            pltpu.SemaphoreType.DMA((blk_count,)),
            pltpu.SemaphoreType.DMA((side_count,)),
            pltpu.SemaphoreType.DMA((side_count,)),
        ],
        compiler_params=pltpu.CompilerParams(
            collective_id=0, has_side_effects=True, vmem_limit_bytes=48 * 1024 * 1024
        ),
    )(
        pair_count,
        pair_source.reshape(1, pairs),
        pair_tile.reshape(1, pairs),
        pair_target.reshape(1, pairs),
        diffusivity,
        column_depth.reshape(1, columns),
        atm_flux,
        tile_bank,
        tracers,
    )
    forced = forced.reshape(subs, half, columns)[:, :fields]
    return (
        mixed
        + response[1][:, None, :] * forced[0][None]
        + response[0][:, None, :] * forced[1][None]
    )


def solution(mesh):
    over = ("sec", "grp", "blk")
    placed = (
        P(None, None, over),
        P(),
        P(over),
        P(over),
        P(over),
        P(over),
        P(None, None, over),
        P(None, over),
        P(over),
    )
    return jax.shard_map(
        body, mesh=mesh, in_specs=placed, out_specs=P(None, None, over), check_vma=False
    )
```

```python
import functools

import jax
import jax.numpy as jnp
from jax import lax
from jax.experimental import pallas as pl
from jax.experimental.pallas import tpu as pltpu
from jax.sharding import PartitionSpec as P

MESH = pl.DeviceIdType.MESH


def up(value, unit):
    return -(-value // unit) * unit


def couple_kernel(
    blk_count,
    grp_count,
    side_count,
    ocean_blocks,
    scale,
    inverse_columns,
    count_ref,
    source_ref,
    tile_ref,
    target_ref,
    diffusivity_ref,
    depth_ref,
    flux_hbm,
    bank_hbm,
    tracers_hbm,
    mixed_ref,
    response_ref,
    forced_ref,
    flux,
    bank,
    tracers,
    given,
    state,
    forced_rows,
    blocks,
    running,
    lists,
    lists_smem,
    outgoing,
    arrived,
    own_total,
    line_totals,
    line_sum,
    side_totals,
    couple,
    weight,
    carry,
    ratio,
    local_sem,
    send_sem,
    recv_sem,
    line_send,
    line_recv,
    side_send,
    side_recv,
):
    sec, grp, blk = lax.axis_index("sec"), lax.axis_index("grp"), lax.axis_index("blk")
    side = sec * grp_count + grp

    def line_peer(step):
        return lax.rem(blk + step, blk_count)

    def side_peer(step):
        return lax.rem(side + step, side_count)

    def line_id(peer):
        return (sec, grp, peer)

    def side_id(peer):
        return (peer // grp_count, lax.rem(peer, grp_count), blk)

    flux_copy = pltpu.make_async_copy(flux_hbm, flux, local_sem.at[0])
    bank_copy = pltpu.make_async_copy(bank_hbm, bank, local_sem.at[1])
    tracers_copy = pltpu.make_async_copy(tracers_hbm, tracers, local_sem.at[2])
    flux_copy.start()
    bank_copy.start()
    tracers_copy.start()

    barrier = pltpu.get_barrier_semaphore()

    @pl.loop(1, blk_count)
    def _(step):
        pl.semaphore_signal(barrier, inc=1, device_id=line_id(line_peer(step)), device_id_type=MESH)

    @pl.loop(1, side_count)
    def _(step):
        pl.semaphore_signal(barrier, inc=1, device_id=side_id(side_peer(step)), device_id_type=MESH)

    pairs = source_ref.shape[1]
    slots = lists.shape[1]
    live_count = count_ref[0]
    square = (pairs, pairs)
    row_at = lax.broadcasted_iota(jnp.int32, square, 0)
    lane_at = lax.broadcasted_iota(jnp.int32, square, 1)
    target_row = jnp.broadcast_to(target_ref[...], square)
    target_col = jnp.transpose(target_row)
    source_col = jnp.transpose(jnp.broadcast_to(source_ref[...], square))
    tile_col = jnp.transpose(jnp.broadcast_to(tile_ref[...], square))
    live_row = lane_at < live_count
    live_col = row_at < live_count
    hits = jnp.where((target_col == lane_at) & live_col, 1, 0)
    counts = jnp.sum(hits, axis=0, keepdims=True)
    padded = jnp.broadcast_to(lax.div(counts + 1, 2) * 2, square)
    before = jnp.where(lane_at < target_col, padded, 0)
    rank = jnp.where((target_row == target_col) & (lane_at < row_at) & live_row, 1, 0)
    slot = jnp.sum(before + rank, axis=1, keepdims=True)
    slot = jnp.where(live_col, jnp.broadcast_to(slot, square), slots)
    block_count = blocks.shape[0] - 1
    steps = running.shape[0] - 1
    lists[...] = jnp.zeros(lists.shape, jnp.int32)
    for first in range(0, slots, pairs):
        lanes = slice(first, first + pairs)
        chosen = slot == lane_at + first
        sources = jnp.sum(jnp.where(chosen, source_col - block_count, 0), axis=0, keepdims=True)
        tiles = jnp.sum(jnp.where(chosen, tile_col, 0), axis=0, keepdims=True)
        targets = jnp.sum(jnp.where(chosen, target_col + 1, 0), axis=0, keepdims=True)
        lists[0:1, lanes] = jnp.clip(sources + block_count, 0, block_count)
        lists[1:2, lanes] = jnp.clip(tiles, 0, bank.shape[0] - 1)
        lists[2:3, lanes] = targets
    upto = jnp.where(row_at <= lane_at, jnp.transpose(padded), 0)
    ends = lax.div(jnp.sum(upto, axis=0, keepdims=True), 2) - 1
    lists[8:9, 0:pairs] = jnp.where(counts > 0, jnp.clip(ends, 0, steps), steps)
    lists_copy = pltpu.make_async_copy(lists, lists_smem, local_sem.at[3])
    lists_copy.start()

    flux_copy.wait()
    fields, subs = flux.shape[0], flux.shape[1]
    rows, width = blocks.shape[1], blocks.shape[2]
    stack = fields * subs
    blocks[...] = jnp.zeros(blocks.shape, blocks.dtype)
    for b in range(block_count):
        blocks[b, 0:stack, :] = flux[:, :, b * width : (b + 1) * width].reshape(stack, width)
    running[steps] = jnp.zeros((rows, width), jnp.float32)
    spread = jnp.zeros((rows, width), jnp.float32)
    for b in range(block_count):
        spread = spread + blocks[b].astype(jnp.float32)
    own_total[...] = spread * scale

    lists_copy.wait()
    bank_copy.wait()

    def add_step(step, held):
        total, last = held
        first, second = 2 * step, 2 * step + 1
        target = lists_smem[2, first]
        left = jnp.concatenate([blocks[lists_smem[0, first]], blocks[lists_smem[0, second]]], axis=1)
        right = jnp.concatenate([bank[lists_smem[1, first]], bank[lists_smem[1, second]]], axis=0)
        keep = jnp.where(target == last, 1.0, 0.0).astype(jnp.float32)
        total = total * keep + jnp.dot(left, right, preferred_element_type=jnp.float32)
        running[step] = total
        return total, target

    lax.fori_loop(
        0, steps, add_step, (jnp.zeros((rows, width), jnp.float32), jnp.int32(-1)), unroll=4
    )

    @pl.loop(0, blk_count)
    def _(peer):
        spread = own_total[...]
        for o in range(ocean_blocks):
            out = running[lists_smem[8, peer * ocean_blocks + o]].astype(jnp.bfloat16)
            outgoing[peer, :, o * width : (o + 1) * width] = out
            spread = spread - out.astype(jnp.float32)
        own_total[...] = spread

    total_row = jnp.sum(jnp.transpose(own_total[...]), axis=0, keepdims=True)
    line_totals[blk] = jnp.broadcast_to(total_row, (8, rows))

    pl.semaphore_wait(barrier, blk_count - 1 + side_count - 1)

    def line_copy(peer, slot_at):
        return pltpu.make_async_remote_copy(
            src_ref=line_totals.at[blk],
            dst_ref=line_totals.at[slot_at],
            send_sem=line_send.at[peer],
            recv_sem=line_recv.at[slot_at],
            device_id=line_id(peer),
            device_id_type=MESH,
        )

    def data_copy(peer, slot_at):
        return pltpu.make_async_remote_copy(
            src_ref=outgoing.at[peer],
            dst_ref=arrived.at[slot_at],
            send_sem=send_sem.at[peer],
            recv_sem=recv_sem.at[slot_at],
            device_id=line_id(peer),
            device_id_type=MESH,
        )

    def side_copy(peer, slot_at):
        return pltpu.make_async_remote_copy(
            src_ref=line_sum,
            dst_ref=side_totals.at[slot_at],
            send_sem=side_send.at[peer],
            recv_sem=side_recv.at[slot_at],
            device_id=side_id(peer),
            device_id_type=MESH,
        )

    @pl.loop(1, blk_count)
    def _(step):
        line_copy(line_peer(step), blk).start()

    @pl.loop(1, blk_count)
    def _(step):
        data_copy(line_peer(step), blk).start()

    fields, levels, columns = tracers.shape
    depth = depth_ref[...]
    level_at = lax.broadcasted_iota(jnp.int32, (levels, columns), 0)
    wet = jnp.where(level_at < depth, 1.0, 0.0)
    couple[0:1, :] = jnp.zeros((1, columns), jnp.float32)
    couple[1:levels, :] = diffusivity_ref[...] * wet[1:levels]
    couple[levels : levels + 1, :] = jnp.zeros((1, columns), jnp.float32)
    previous = jnp.zeros((1, columns), jnp.float32)
    for k in range(levels):
        a = couple[k : k + 1, :]
        b = couple[k + 1 : k + 2, :]
        inverse = 1.0 / (1.0 + a + b - a * previous)
        previous = b * inverse
        weight[k : k + 1, :] = jnp.where(depth > k, inverse, 0.0)
        carry[k : k + 1, :] = a * inverse
        ratio[k : k + 1, :] = previous
    for sweep in range(2):
        right = response_ref.at[0]
        unit = jnp.zeros((1, columns), jnp.float32)
        forward = []
        for k in range(levels):
            if sweep == 0:
                pushed = weight[0:1, :] if k == 0 else jnp.zeros((1, columns), jnp.float32)
            else:
                pushed = right[k : k + 1, :] * weight[k : k + 1, :]
            unit = pushed + carry[k : k + 1, :] * unit
            forward.append(unit)
        solved = forward[-1]
        response_ref[sweep, levels - 1 : levels, :] = solved
        for k in range(levels - 2, -1, -1):
            solved = forward[k] + ratio[k : k + 1, :] * solved
            response_ref[sweep, k : k + 1, :] = solved

    tracers_copy.wait()

    @pl.loop(0, fields)
    def _(f):
        at = pl.ds(pl.multiple_of(f * levels, levels), levels)
        for o in range(ocean_blocks):
            lanes = slice(o * width, (o + 1) * width)
            given[o, at, :] = tracers[f, :, lanes].astype(jnp.float32)

    def level_rows(k):
        return pl.ds(k, fields, stride=levels)

    def put_level(k, held):
        for o in range(ocean_blocks):
            mixed_ref[o, level_rows(k), :] = held[:, o * width : (o + 1) * width]

    def first_level(k, held):
        read = [given[o, level_rows(k), :] for o in range(ocean_blocks)]
        held = jnp.concatenate(read, axis=1) * weight[pl.ds(k, 1), :] + carry[pl.ds(k, 1), :] * held
        state[k] = held
        return held

    def forward_level(k, held):
        held = state[k] * weight[pl.ds(k, 1), :] + carry[pl.ds(k, 1), :] * held
        state[k] = held
        return held

    def back_level(i, held):
        k = levels - 2 - i
        held = state[k] + ratio[pl.ds(k, 1), :] * held
        state[k] = held
        return held

    def last_level(i, held):
        k = levels - 2 - i
        held = state[k] + ratio[pl.ds(k, 1), :] * held
        put_level(k, held)
        return held

    nothing = jnp.zeros((fields, columns), jnp.float32)
    bottom = lax.fori_loop(0, levels, first_level, nothing, unroll=4)

    @pl.loop(1, blk_count)
    def _(step):
        peer = line_peer(step)
        line_copy(peer, peer).wait_recv()

    summed = line_totals[0]
    for p in range(1, blk_count):
        summed = summed + line_totals[p]
    line_sum[...] = summed

    @pl.loop(1, side_count)
    def _(step):
        side_copy(side_peer(step), side).start()

    lax.fori_loop(0, levels - 1, back_level, bottom)
    bottom = lax.fori_loop(0, levels, forward_level, nothing, unroll=4)
    put_level(levels - 1, bottom)
    lax.fori_loop(0, levels - 1, last_level, bottom)

    @pl.loop(1, side_count)
    def _(step):
        peer = side_peer(step)
        side_copy(peer, peer).wait_recv()

    side_totals[side] = line_sum[...]
    everything = side_totals[0]
    for p in range(1, side_count):
        everything = everything + side_totals[p]
    correction = jnp.transpose(jnp.broadcast_to(everything[0:1, :] * inverse_columns, (rows, rows)))

    @pl.loop(1, blk_count)
    def _(step):
        peer = line_peer(step)
        data_copy(peer, peer).wait_recv()

    arrived[blk] = outgoing[blk]
    for o in range(ocean_blocks):
        lanes = slice(o * width, (o + 1) * width)
        forced = arrived[0, :, lanes].astype(jnp.float32)
        for p in range(1, blk_count):
            forced = forced + arrived[p, :, lanes].astype(jnp.float32)
        forced_rows[o] = forced + correction
        for s in range(subs):
            forced_ref[s, :, lanes] = forced_rows[o, pl.ds(s, fields, stride=subs), :]

    @pl.loop(1, blk_count)
    def _(step):
        peer = line_peer(step)
        line_copy(peer, blk).wait_send()
        data_copy(peer, blk).wait_send()

    @pl.loop(1, side_count)
    def _(step):
        side_copy(side_peer(step), side).wait_send()


def join_kernel(parts, mixed_ref, response_ref, forced_ref, result_hbm, result, sems):
    fields, levels, columns = result.shape
    halves, _, width = mixed_ref.shape
    near, far = response_ref[0], response_ref[1]
    part = fields // parts

    def copy(n):
        at = pl.ds(n * part, part)
        return pltpu.make_async_copy(result.at[at], result_hbm.at[at], sems.at[n])

    for n in range(parts):

        @pl.loop(n * part, (n + 1) * part)
        def _(f):
            at = pl.ds(pl.multiple_of(f * levels, levels), levels)
            mixed = jnp.concatenate([mixed_ref[o, at, :] for o in range(halves)], axis=1)
            early = forced_ref[0, pl.ds(f, 1), :]
            late = forced_ref[1, pl.ds(f, 1), :]
            result[f] = mixed + far * early + near * late

        copy(n).start()
    for n in range(parts):
        copy(n).wait()


def body(
    atm_flux,
    tile_bank,
    pair_count,
    pair_source,
    pair_tile,
    pair_target,
    tracers,
    diffusivity,
    column_depth,
):
    subs, fields, atm_rows = atm_flux.shape
    width = tile_bank.shape[1]
    block_count = atm_rows // width
    levels, _, columns = tracers.shape
    ocean_blocks = columns // width
    blk_count, grp_count = lax.axis_size("blk"), lax.axis_size("grp")
    side_count = lax.axis_size("sec") * grp_count
    pairs = pair_source.shape[0]
    rows = up(subs * fields, 128)
    slot_count = up(pairs + blk_count * ocean_blocks, 2)
    steps = slot_count // 2
    steps_up = up(steps, 4)
    slots = up(2 * steps_up, 128)
    f32, bf16 = jnp.float32, jnp.bfloat16
    vmem = pl.BlockSpec(memory_space=pltpu.VMEM)
    smem = pl.BlockSpec(memory_space=pltpu.SMEM)
    anywhere = pl.BlockSpec(memory_space=pl.ANY)
    mixed, response, forced = pl.pallas_call(
        functools.partial(
            couple_kernel,
            blk_count,
            grp_count,
            side_count,
            ocean_blocks,
            ocean_blocks / block_count,
            1.0 / (columns * blk_count * side_count),
        ),
        out_shape=(
            jax.ShapeDtypeStruct((ocean_blocks, fields * levels, width), f32),
            jax.ShapeDtypeStruct((2, levels, columns), f32),
            jax.ShapeDtypeStruct((subs, fields, columns), f32),
        ),
        in_specs=[smem, vmem, vmem, vmem, vmem, vmem, anywhere, anywhere, anywhere],
        out_specs=(vmem, vmem, vmem),
        scratch_shapes=[
            pltpu.VMEM((fields, subs, atm_rows), bf16),
            pltpu.VMEM(tile_bank.shape, bf16),
            pltpu.VMEM((fields, levels, columns), bf16),
            pltpu.VMEM((ocean_blocks, fields * levels, width), f32),
            pltpu.VMEM((levels, fields, columns), f32),
            pltpu.VMEM((ocean_blocks, rows, width), f32),
            pltpu.VMEM((block_count + 1, rows, width), bf16),
            pltpu.VMEM((steps_up + 1, rows, width), f32),
            pltpu.VMEM((16, slots), jnp.int32),
            pltpu.SMEM((16, slots), jnp.int32),
            pltpu.VMEM((blk_count, rows, columns), bf16),
            pltpu.VMEM((blk_count, rows, columns), bf16),
            pltpu.VMEM((rows, width), f32),
            pltpu.VMEM((blk_count, 8, rows), f32),
            pltpu.VMEM((8, rows), f32),
            pltpu.VMEM((side_count, 8, rows), f32),
            pltpu.VMEM((levels + 8, columns), f32),
            pltpu.VMEM((levels, columns), f32),
            pltpu.VMEM((levels, columns), f32),
            pltpu.VMEM((levels, columns), f32),
            pltpu.SemaphoreType.DMA((5,)),
            pltpu.SemaphoreType.DMA((blk_count,)),
            pltpu.SemaphoreType.DMA((blk_count,)),
            pltpu.SemaphoreType.DMA((blk_count,)),
            pltpu.SemaphoreType.DMA((blk_count,)),
            pltpu.SemaphoreType.DMA((side_count,)),
            pltpu.SemaphoreType.DMA((side_count,)),
        ],
        compiler_params=pltpu.CompilerParams(
            collective_id=0, has_side_effects=True, vmem_limit_bytes=48 * 1024 * 1024
        ),
    )(
        pair_count,
        pair_source.reshape(1, pairs),
        pair_tile.reshape(1, pairs),
        pair_target.reshape(1, pairs),
        diffusivity,
        column_depth.reshape(1, columns),
        jnp.transpose(atm_flux, (1, 0, 2)),
        tile_bank,
        jnp.transpose(tracers, (1, 0, 2)),
    )
    parts = 4 if fields % 4 == 0 else 1
    result = pl.pallas_call(
        functools.partial(join_kernel, parts),
        out_shape=jax.ShapeDtypeStruct((fields, levels, columns), f32),
        in_specs=[vmem, vmem, vmem],
        out_specs=anywhere,
        scratch_shapes=[
            pltpu.VMEM((fields, levels, columns), f32),
            pltpu.SemaphoreType.DMA((parts,)),
        ],
        compiler_params=pltpu.CompilerParams(vmem_limit_bytes=16 * 1024 * 1024),
    )(mixed, response, forced)
    return jnp.transpose(result, (1, 0, 2))


def solution(mesh):
    over = ("sec", "grp", "blk")
    placed = (
        P(None, None, over),
        P(),
        P(over),
        P(over),
        P(over),
        P(over),
        P(None, None, over),
        P(None, over),
        P(over),
    )
    return jax.shard_map(
        body, mesh=mesh, in_specs=placed, out_specs=P(None, None, over), check_vma=False
    )
```

```python
import functools

import jax
import jax.numpy as jnp
from jax import lax
from jax.experimental import pallas as pl
from jax.experimental.pallas import tpu as pltpu
from jax.sharding import PartitionSpec as P

MESH = pl.DeviceIdType.MESH


def up(value, unit):
    return -(-value // unit) * unit


def couple_kernel(
    blk_count,
    grp_count,
    side_count,
    ocean_blocks,
    scale,
    inverse_columns,
    count_ref,
    source_hbm,
    tile_hbm,
    target_hbm,
    diffusivity_hbm,
    depth_hbm,
    flux_hbm,
    bank_hbm,
    tracers_hbm,
    mixed_ref,
    response_ref,
    forced_ref,
    source_ref,
    tile_ref,
    target_ref,
    diffusivity_ref,
    depth_ref,
    flux,
    bank,
    tracers,
    given,
    state,
    forced_rows,
    blocks,
    running,
    lists,
    lists_smem,
    outgoing,
    arrived,
    own_total,
    line_totals,
    line_sum,
    side_totals,
    couple,
    weight,
    carry,
    ratio,
    local_sem,
    send_sem,
    recv_sem,
    line_send,
    line_recv,
    side_send,
    side_recv,
):
    sec, grp, blk = lax.axis_index("sec"), lax.axis_index("grp"), lax.axis_index("blk")
    side = sec * grp_count + grp

    def line_peer(step):
        return lax.rem(blk + step, blk_count)

    def side_peer(step):
        return lax.rem(side + step, side_count)

    def line_id(peer):
        return (sec, grp, peer)

    def side_id(peer):
        return (peer // grp_count, lax.rem(peer, grp_count), blk)

    small_copies = [
        pltpu.make_async_copy(given_hbm, ref, local_sem.at[4 + i])
        for i, (given_hbm, ref) in enumerate(
            (
                (target_hbm, target_ref),
                (source_hbm, source_ref),
                (tile_hbm, tile_ref),
                (depth_hbm, depth_ref),
                (diffusivity_hbm, diffusivity_ref),
            )
        )
    ]
    for small in small_copies[:3]:
        small.start()
    flux_copy = pltpu.make_async_copy(flux_hbm, flux, local_sem.at[0])
    bank_copy = pltpu.make_async_copy(bank_hbm, bank, local_sem.at[1])
    tracers_copy = pltpu.make_async_copy(tracers_hbm, tracers, local_sem.at[2])
    flux_copy.start()
    bank_copy.start()
    for small in small_copies[3:]:
        small.start()
    tracers_copy.start()

    barrier = pltpu.get_barrier_semaphore()

    @pl.loop(1, blk_count)
    def _(step):
        pl.semaphore_signal(barrier, inc=1, device_id=line_id(line_peer(step)), device_id_type=MESH)

    @pl.loop(1, side_count)
    def _(step):
        pl.semaphore_signal(barrier, inc=1, device_id=side_id(side_peer(step)), device_id_type=MESH)

    pairs = source_ref.shape[1]
    slots = lists.shape[1]
    for small in small_copies[:3]:
        small.wait()
    live_count = count_ref[0]
    square = (pairs, pairs)
    row_at = lax.broadcasted_iota(jnp.int32, square, 0)
    lane_at = lax.broadcasted_iota(jnp.int32, square, 1)
    target_row = jnp.broadcast_to(target_ref[...], square)
    target_col = jnp.transpose(target_row)
    source_col = jnp.transpose(jnp.broadcast_to(source_ref[...], square))
    tile_col = jnp.transpose(jnp.broadcast_to(tile_ref[...], square))
    live_row = lane_at < live_count
    live_col = row_at < live_count
    hits = jnp.where((target_col == lane_at) & live_col, 1, 0)
    counts = jnp.sum(hits, axis=0, keepdims=True)
    padded = jnp.broadcast_to(lax.div(counts + 1, 2) * 2, square)
    before = jnp.where(lane_at < target_col, padded, 0)
    rank = jnp.where((target_row == target_col) & (lane_at < row_at) & live_row, 1, 0)
    slot = jnp.sum(before + rank, axis=1, keepdims=True)
    slot = jnp.where(live_col, jnp.broadcast_to(slot, square), slots)
    block_count = blocks.shape[0] - 1
    steps = running.shape[0] - 1
    lists[...] = jnp.zeros(lists.shape, jnp.int32)
    for first in range(0, slots, pairs):
        lanes = slice(first, first + pairs)
        chosen = slot == lane_at + first
        sources = jnp.sum(jnp.where(chosen, source_col - block_count, 0), axis=0, keepdims=True)
        tiles = jnp.sum(jnp.where(chosen, tile_col, 0), axis=0, keepdims=True)
        targets = jnp.sum(jnp.where(chosen, target_col + 1, 0), axis=0, keepdims=True)
        lists[0:1, lanes] = jnp.clip(sources + block_count, 0, block_count)
        lists[1:2, lanes] = jnp.clip(tiles, 0, bank.shape[0] - 1)
        lists[2:3, lanes] = targets
    upto = jnp.where(row_at <= lane_at, jnp.transpose(padded), 0)
    ends = lax.div(jnp.sum(upto, axis=0, keepdims=True), 2) - 1
    lists[8:9, 0:pairs] = jnp.where(counts > 0, jnp.clip(ends, 0, steps), steps)
    lists_copy = pltpu.make_async_copy(lists, lists_smem, local_sem.at[3])
    lists_copy.start()

    flux_copy.wait()
    fields, subs = flux.shape[0], flux.shape[1]
    rows, width = blocks.shape[1], blocks.shape[2]
    stack = fields * subs
    blocks[...] = jnp.zeros(blocks.shape, blocks.dtype)
    for b in range(block_count):
        blocks[b, 0:stack, :] = flux[:, :, b * width : (b + 1) * width].reshape(stack, width)
    running[steps] = jnp.zeros((rows, width), jnp.float32)
    spread = jnp.zeros((rows, width), jnp.float32)
    for b in range(block_count):
        spread = spread + blocks[b].astype(jnp.float32)
    own_total[...] = spread * scale

    lists_copy.wait()
    bank_copy.wait()

    def add_step(step, held):
        total, last = held
        first, second = 2 * step, 2 * step + 1
        target = lists_smem[2, first]
        left = jnp.concatenate([blocks[lists_smem[0, first]], blocks[lists_smem[0, second]]], axis=1)
        right = jnp.concatenate([bank[lists_smem[1, first]], bank[lists_smem[1, second]]], axis=0)
        keep = jnp.where(target == last, 1.0, 0.0).astype(jnp.float32)
        total = total * keep + jnp.dot(left, right, preferred_element_type=jnp.float32)
        running[step] = total
        return total, target

    lax.fori_loop(
        0, steps, add_step, (jnp.zeros((rows, width), jnp.float32), jnp.int32(-1)), unroll=4
    )

    @pl.loop(0, blk_count)
    def _(peer):
        spread = own_total[...]
        for o in range(ocean_blocks):
            out = running[lists_smem[8, peer * ocean_blocks + o]].astype(jnp.bfloat16)
            outgoing[peer, :, o * width : (o + 1) * width] = out
            spread = spread - out.astype(jnp.float32)
        own_total[...] = spread

    total_row = jnp.sum(jnp.transpose(own_total[...]), axis=0, keepdims=True)
    line_totals[blk] = jnp.broadcast_to(total_row, (8, rows))

    pl.semaphore_wait(barrier, blk_count - 1 + side_count - 1)

    def line_copy(peer, slot_at):
        return pltpu.make_async_remote_copy(
            src_ref=line_totals.at[blk],
            dst_ref=line_totals.at[slot_at],
            send_sem=line_send.at[peer],
            recv_sem=line_recv.at[slot_at],
            device_id=line_id(peer),
            device_id_type=MESH,
        )

    def data_copy(peer, slot_at):
        return pltpu.make_async_remote_copy(
            src_ref=outgoing.at[peer],
            dst_ref=arrived.at[slot_at],
            send_sem=send_sem.at[peer],
            recv_sem=recv_sem.at[slot_at],
            device_id=line_id(peer),
            device_id_type=MESH,
        )

    def side_copy(peer, slot_at):
        return pltpu.make_async_remote_copy(
            src_ref=line_sum,
            dst_ref=side_totals.at[slot_at],
            send_sem=side_send.at[peer],
            recv_sem=side_recv.at[slot_at],
            device_id=side_id(peer),
            device_id_type=MESH,
        )

    @pl.loop(1, blk_count)
    def _(step):
        line_copy(line_peer(step), blk).start()

    @pl.loop(1, blk_count)
    def _(step):
        data_copy(line_peer(step), blk).start()

    fields, levels, columns = tracers.shape
    for small in small_copies[3:]:
        small.wait()
    depth = depth_ref[...]
    level_at = lax.broadcasted_iota(jnp.int32, (levels, columns), 0)
    wet = jnp.where(level_at < depth, 1.0, 0.0)
    couple[0:1, :] = jnp.zeros((1, columns), jnp.float32)
    couple[1:levels, :] = diffusivity_ref[...] * wet[1:levels]
    couple[levels : levels + 1, :] = jnp.zeros((1, columns), jnp.float32)
    previous = jnp.zeros((1, columns), jnp.float32)
    for k in range(levels):
        a = couple[k : k + 1, :]
        b = couple[k + 1 : k + 2, :]
        inverse = 1.0 / (1.0 + a + b - a * previous)
        previous = b * inverse
        weight[k : k + 1, :] = jnp.where(depth > k, inverse, 0.0)
        carry[k : k + 1, :] = a * inverse
        ratio[k : k + 1, :] = previous
    for sweep in range(2):
        right = response_ref.at[0]
        unit = jnp.zeros((1, columns), jnp.float32)
        forward = []
        for k in range(levels):
            if sweep == 0:
                pushed = weight[0:1, :] if k == 0 else jnp.zeros((1, columns), jnp.float32)
            else:
                pushed = right[k : k + 1, :] * weight[k : k + 1, :]
            unit = pushed + carry[k : k + 1, :] * unit
            forward.append(unit)
        solved = forward[-1]
        response_ref[sweep, levels - 1 : levels, :] = solved
        for k in range(levels - 2, -1, -1):
            solved = forward[k] + ratio[k : k + 1, :] * solved
            response_ref[sweep, k : k + 1, :] = solved

    tracers_copy.wait()

    @pl.loop(0, fields)
    def _(f):
        at = pl.ds(pl.multiple_of(f * levels, levels), levels)
        for o in range(ocean_blocks):
            lanes = slice(o * width, (o + 1) * width)
            given[o, at, :] = tracers[f, :, lanes].astype(jnp.float32)

    def level_rows(k):
        return pl.ds(k, fields, stride=levels)

    def put_level(k, held):
        for o in range(ocean_blocks):
            mixed_ref[o, level_rows(k), :] = held[:, o * width : (o + 1) * width]

    def first_level(k, held):
        read = [given[o, level_rows(k), :] for o in range(ocean_blocks)]
        held = jnp.concatenate(read, axis=1) * weight[pl.ds(k, 1), :] + carry[pl.ds(k, 1), :] * held
        state[k] = held
        return held

    def forward_level(k, held):
        held = state[k] * weight[pl.ds(k, 1), :] + carry[pl.ds(k, 1), :] * held
        state[k] = held
        return held

    def back_level(i, held):
        k = levels - 2 - i
        held = state[k] + ratio[pl.ds(k, 1), :] * held
        state[k] = held
        return held

    def last_level(i, held):
        k = levels - 2 - i
        held = state[k] + ratio[pl.ds(k, 1), :] * held
        put_level(k, held)
        return held

    nothing = jnp.zeros((fields, columns), jnp.float32)
    bottom = lax.fori_loop(0, levels, first_level, nothing, unroll=4)

    @pl.loop(1, blk_count)
    def _(step):
        peer = line_peer(step)
        line_copy(peer, peer).wait_recv()

    summed = line_totals[0]
    for p in range(1, blk_count):
        summed = summed + line_totals[p]
    line_sum[...] = summed

    @pl.loop(1, side_count)
    def _(step):
        side_copy(side_peer(step), side).start()

    lax.fori_loop(0, levels - 1, back_level, bottom)
    bottom = lax.fori_loop(0, levels, forward_level, nothing, unroll=4)
    put_level(levels - 1, bottom)
    lax.fori_loop(0, levels - 1, last_level, bottom)

    @pl.loop(1, side_count)
    def _(step):
        peer = side_peer(step)
        side_copy(peer, peer).wait_recv()

    side_totals[side] = line_sum[...]
    everything = side_totals[0]
    for p in range(1, side_count):
        everything = everything + side_totals[p]
    correction = jnp.transpose(jnp.broadcast_to(everything[0:1, :] * inverse_columns, (rows, rows)))

    @pl.loop(1, blk_count)
    def _(step):
        peer = line_peer(step)
        data_copy(peer, peer).wait_recv()

    arrived[blk] = outgoing[blk]
    for o in range(ocean_blocks):
        lanes = slice(o * width, (o + 1) * width)
        forced = arrived[0, :, lanes].astype(jnp.float32)
        for p in range(1, blk_count):
            forced = forced + arrived[p, :, lanes].astype(jnp.float32)
        forced_rows[o] = forced + correction
        for s in range(subs):
            forced_ref[s, :, lanes] = forced_rows[o, pl.ds(s, fields, stride=subs), :]

    @pl.loop(1, blk_count)
    def _(step):
        peer = line_peer(step)
        line_copy(peer, blk).wait_send()
        data_copy(peer, blk).wait_send()

    @pl.loop(1, side_count)
    def _(step):
        side_copy(side_peer(step), side).wait_send()


def join_kernel(parts, mixed_ref, response_ref, forced_ref, result_hbm, result, sems):
    fields, levels, columns = result.shape
    halves, _, width = mixed_ref.shape
    near, far = response_ref[0], response_ref[1]
    part = fields // parts

    def copy(n):
        at = pl.ds(n * part, part)
        return pltpu.make_async_copy(result.at[at], result_hbm.at[at], sems.at[n])

    for n in range(parts):

        @pl.loop(n * part, (n + 1) * part)
        def _(f):
            at = pl.ds(pl.multiple_of(f * levels, levels), levels)
            mixed = jnp.concatenate([mixed_ref[o, at, :] for o in range(halves)], axis=1)
            early = forced_ref[0, pl.ds(f, 1), :]
            late = forced_ref[1, pl.ds(f, 1), :]
            result[f] = mixed + far * early + near * late

        copy(n).start()
    for n in range(parts):
        copy(n).wait()


def body(
    atm_flux,
    tile_bank,
    pair_count,
    pair_source,
    pair_tile,
    pair_target,
    tracers,
    diffusivity,
    column_depth,
):
    subs, fields, atm_rows = atm_flux.shape
    width = tile_bank.shape[1]
    block_count = atm_rows // width
    levels, _, columns = tracers.shape
    ocean_blocks = columns // width
    blk_count, grp_count = lax.axis_size("blk"), lax.axis_size("grp")
    side_count = lax.axis_size("sec") * grp_count
    pairs = pair_source.shape[0]
    rows = up(subs * fields, 128)
    slot_count = up(pairs + blk_count * ocean_blocks, 2)
    steps = slot_count // 2
    steps_up = up(steps, 4)
    slots = up(2 * steps_up, 128)
    f32, bf16 = jnp.float32, jnp.bfloat16
    vmem = pl.BlockSpec(memory_space=pltpu.VMEM)
    anywhere = pl.BlockSpec(memory_space=pl.ANY)
    mixed, response, forced = pl.pallas_call(
        functools.partial(
            couple_kernel,
            blk_count,
            grp_count,
            side_count,
            ocean_blocks,
            ocean_blocks / block_count,
            1.0 / (columns * blk_count * side_count),
        ),
        out_shape=(
            jax.ShapeDtypeStruct((ocean_blocks, fields * levels, width), f32),
            jax.ShapeDtypeStruct((2, levels, columns), f32),
            jax.ShapeDtypeStruct((subs, fields, columns), f32),
        ),
        in_specs=[pl.BlockSpec(memory_space=pltpu.SMEM)]
        + [pl.BlockSpec(memory_space=pltpu.HBM)] * 8,
        out_specs=(vmem, vmem, vmem),
        scratch_shapes=[
            pltpu.VMEM((1, pairs), jnp.int32),
            pltpu.VMEM((1, pairs), jnp.int32),
            pltpu.VMEM((1, pairs), jnp.int32),
            pltpu.VMEM((levels - 1, columns), f32),
            pltpu.VMEM((1, columns), jnp.int32),
            pltpu.VMEM((fields, subs, atm_rows), bf16),
            pltpu.VMEM(tile_bank.shape, bf16),
            pltpu.VMEM((fields, levels, columns), bf16),
            pltpu.VMEM((ocean_blocks, fields * levels, width), f32),
            pltpu.VMEM((levels, fields, columns), f32),
            pltpu.VMEM((ocean_blocks, rows, width), f32),
            pltpu.VMEM((block_count + 1, rows, width), bf16),
            pltpu.VMEM((steps_up + 1, rows, width), f32),
            pltpu.VMEM((16, slots), jnp.int32),
            pltpu.SMEM((16, slots), jnp.int32),
            pltpu.VMEM((blk_count, rows, columns), bf16),
            pltpu.VMEM((blk_count, rows, columns), bf16),
            pltpu.VMEM((rows, width), f32),
            pltpu.VMEM((blk_count, 8, rows), f32),
            pltpu.VMEM((8, rows), f32),
            pltpu.VMEM((side_count, 8, rows), f32),
            pltpu.VMEM((levels + 8, columns), f32),
            pltpu.VMEM((levels, columns), f32),
            pltpu.VMEM((levels, columns), f32),
            pltpu.VMEM((levels, columns), f32),
            pltpu.SemaphoreType.DMA((9,)),
            pltpu.SemaphoreType.DMA((blk_count,)),
            pltpu.SemaphoreType.DMA((blk_count,)),
            pltpu.SemaphoreType.DMA((blk_count,)),
            pltpu.SemaphoreType.DMA((blk_count,)),
            pltpu.SemaphoreType.DMA((side_count,)),
            pltpu.SemaphoreType.DMA((side_count,)),
        ],
        compiler_params=pltpu.CompilerParams(
            collective_id=0, has_side_effects=True, vmem_limit_bytes=48 * 1024 * 1024
        ),
    )(
        pair_count,
        *[
            pltpu.with_memory_space_constraint(operand, pltpu.HBM)
            for operand in (
                pair_source.reshape(1, pairs),
                pair_tile.reshape(1, pairs),
                pair_target.reshape(1, pairs),
                diffusivity,
                column_depth.reshape(1, columns),
                jnp.transpose(atm_flux, (1, 0, 2)),
                tile_bank,
                jnp.transpose(tracers, (1, 0, 2)),
            )
        ]
    )
    parts = 4 if fields % 4 == 0 else 1
    result = pl.pallas_call(
        functools.partial(join_kernel, parts),
        out_shape=jax.ShapeDtypeStruct((fields, levels, columns), f32),
        in_specs=[vmem, vmem, vmem],
        out_specs=anywhere,
        scratch_shapes=[
            pltpu.VMEM((fields, levels, columns), f32),
            pltpu.SemaphoreType.DMA((parts,)),
        ],
        compiler_params=pltpu.CompilerParams(vmem_limit_bytes=16 * 1024 * 1024),
    )(mixed, response, forced)
    return jnp.transpose(result, (1, 0, 2))


def solution(mesh):
    over = ("sec", "grp", "blk")
    placed = (
        P(None, None, over),
        P(),
        P(over),
        P(over),
        P(over),
        P(over),
        P(None, None, over),
        P(None, over),
        P(over),
    )
    return jax.shard_map(
        body, mesh=mesh, in_specs=placed, out_specs=P(None, None, over), check_vma=False
    )
```

```python
import functools

import jax
import jax.numpy as jnp
from jax import lax
from jax.experimental import pallas as pl
from jax.experimental.pallas import tpu as pltpu
from jax.sharding import PartitionSpec as P

MESH = pl.DeviceIdType.MESH


def up(value, unit):
    return -(-value // unit) * unit


def couple_kernel(
    blk_count,
    grp_count,
    side_count,
    ocean_blocks,
    scale,
    inverse_columns,
    count_ref,
    source_hbm,
    tile_hbm,
    target_hbm,
    diffusivity_hbm,
    depth_hbm,
    flux_hbm,
    bank_hbm,
    tracers_hbm,
    mixed_ref,
    response_ref,
    forced_ref,
    source_ref,
    tile_ref,
    target_ref,
    diffusivity_ref,
    depth_ref,
    flux,
    bank,
    tracers,
    given,
    state,
    forced_rows,
    blocks,
    running,
    lists,
    lists_smem,
    outgoing,
    arrived,
    own_total,
    line_totals,
    line_sum,
    side_totals,
    couple,
    weight,
    carry,
    ratio,
    local_sem,
    send_sem,
    recv_sem,
    line_send,
    line_recv,
    side_send,
    side_recv,
):
    sec, grp, blk = lax.axis_index("sec"), lax.axis_index("grp"), lax.axis_index("blk")
    side = sec * grp_count + grp

    def line_peer(step):
        return lax.rem(blk + step, blk_count)

    def side_peer(step):
        return lax.rem(side + step, side_count)

    def line_id(peer):
        return (sec, grp, peer)

    def side_id(peer):
        return (peer // grp_count, lax.rem(peer, grp_count), blk)

    small_copies = [
        pltpu.make_async_copy(given_hbm, ref, local_sem.at[4 + i])
        for i, (given_hbm, ref) in enumerate(
            (
                (target_hbm, target_ref),
                (source_hbm, source_ref),
                (tile_hbm, tile_ref),
                (depth_hbm, depth_ref),
                (diffusivity_hbm, diffusivity_ref),
            )
        )
    ]
    for small in small_copies[:3]:
        small.start()
    flux_copy = pltpu.make_async_copy(flux_hbm, flux, local_sem.at[0])
    bank_copy = pltpu.make_async_copy(bank_hbm, bank, local_sem.at[1])
    tracers_copy = pltpu.make_async_copy(tracers_hbm, tracers, local_sem.at[2])
    flux_copy.start()
    bank_copy.start()
    for small in small_copies[3:]:
        small.start()
    tracers_copy.start()

    barrier = pltpu.get_barrier_semaphore()

    @pl.loop(1, blk_count)
    def _(step):
        pl.semaphore_signal(barrier, inc=1, device_id=line_id(line_peer(step)), device_id_type=MESH)

    @pl.loop(1, side_count)
    def _(step):
        pl.semaphore_signal(barrier, inc=1, device_id=side_id(side_peer(step)), device_id_type=MESH)

    pairs = source_ref.shape[1]
    slots = lists.shape[1]
    for small in small_copies[:3]:
        small.wait()
    live_count = count_ref[0]
    square = (pairs, pairs)
    row_at = lax.broadcasted_iota(jnp.int32, square, 0)
    lane_at = lax.broadcasted_iota(jnp.int32, square, 1)
    target_row = jnp.broadcast_to(target_ref[...], square)
    target_col = jnp.transpose(target_row)
    source_col = jnp.transpose(jnp.broadcast_to(source_ref[...], square))
    tile_col = jnp.transpose(jnp.broadcast_to(tile_ref[...], square))
    live_row = lane_at < live_count
    live_col = row_at < live_count
    hits = jnp.where((target_col == lane_at) & live_col, 1, 0)
    counts = jnp.sum(hits, axis=0, keepdims=True)
    padded = jnp.broadcast_to(lax.div(counts + 1, 2) * 2, square)
    before = jnp.where(lane_at < target_col, padded, 0)
    rank = jnp.where((target_row == target_col) & (lane_at < row_at) & live_row, 1, 0)
    slot = jnp.sum(before + rank, axis=1, keepdims=True)
    slot = jnp.where(live_col, jnp.broadcast_to(slot, square), slots)
    block_count = blocks.shape[0] - 1
    steps = running.shape[0] - 1
    lists[...] = jnp.zeros(lists.shape, jnp.int32)
    for first in range(0, slots, pairs):
        lanes = slice(first, first + pairs)
        chosen = slot == lane_at + first
        sources = jnp.sum(jnp.where(chosen, source_col - block_count, 0), axis=0, keepdims=True)
        tiles = jnp.sum(jnp.where(chosen, tile_col, 0), axis=0, keepdims=True)
        targets = jnp.sum(jnp.where(chosen, target_col + 1, 0), axis=0, keepdims=True)
        lists[0:1, lanes] = jnp.clip(sources + block_count, 0, block_count)
        lists[1:2, lanes] = jnp.clip(tiles, 0, bank.shape[0] - 1)
        lists[2:3, lanes] = targets
    upto = jnp.where(row_at <= lane_at, jnp.transpose(padded), 0)
    ends = lax.div(jnp.sum(upto, axis=0, keepdims=True), 2) - 1
    lists[8:9, 0:pairs] = jnp.where(counts > 0, jnp.clip(ends, 0, steps), steps)
    lists_copy = pltpu.make_async_copy(lists, lists_smem, local_sem.at[3])
    lists_copy.start()

    flux_copy.wait()
    fields, subs = flux.shape[0], flux.shape[1]
    rows, width = blocks.shape[1], blocks.shape[2]
    stack = fields * subs
    blocks[...] = jnp.zeros(blocks.shape, blocks.dtype)
    for b in range(block_count):
        blocks[b, 0:stack, :] = flux[:, :, b * width : (b + 1) * width].reshape(stack, width)
    running[steps] = jnp.zeros((rows, width), jnp.float32)
    spread = jnp.zeros((rows, width), jnp.float32)
    for b in range(block_count):
        spread = spread + blocks[b].astype(jnp.float32)
    own_total[...] = spread * scale

    lists_copy.wait()
    bank_copy.wait()

    def add_step(step, held):
        total, last = held
        first, second = 2 * step, 2 * step + 1
        target = lists_smem[2, first]
        left = jnp.concatenate([blocks[lists_smem[0, first]], blocks[lists_smem[0, second]]], axis=1)
        right = jnp.concatenate([bank[lists_smem[1, first]], bank[lists_smem[1, second]]], axis=0)
        keep = jnp.where(target == last, 1.0, 0.0).astype(jnp.float32)
        total = total * keep + jnp.dot(left, right, preferred_element_type=jnp.float32)
        running[step] = total
        return total, target

    lax.fori_loop(
        0, steps, add_step, (jnp.zeros((rows, width), jnp.float32), jnp.int32(-1)), unroll=steps // 4
    )

    @pl.loop(0, blk_count)
    def _(peer):
        spread = own_total[...]
        for o in range(ocean_blocks):
            out = running[lists_smem[8, peer * ocean_blocks + o]].astype(jnp.bfloat16)
            outgoing[peer, :, o * width : (o + 1) * width] = out
            spread = spread - out.astype(jnp.float32)
        own_total[...] = spread

    total_row = jnp.sum(jnp.transpose(own_total[...]), axis=0, keepdims=True)
    line_totals[blk] = jnp.broadcast_to(total_row, (8, rows))

    pl.semaphore_wait(barrier, blk_count - 1 + side_count - 1)

    def line_copy(peer, slot_at):
        return pltpu.make_async_remote_copy(
            src_ref=line_totals.at[blk],
            dst_ref=line_totals.at[slot_at],
            send_sem=line_send.at[peer],
            recv_sem=line_recv.at[slot_at],
            device_id=line_id(peer),
            device_id_type=MESH,
        )

    def data_copy(peer, slot_at):
        return pltpu.make_async_remote_copy(
            src_ref=outgoing.at[peer],
            dst_ref=arrived.at[slot_at],
            send_sem=send_sem.at[peer],
            recv_sem=recv_sem.at[slot_at],
            device_id=line_id(peer),
            device_id_type=MESH,
        )

    def side_copy(peer, slot_at):
        return pltpu.make_async_remote_copy(
            src_ref=line_sum,
            dst_ref=side_totals.at[slot_at],
            send_sem=side_send.at[peer],
            recv_sem=side_recv.at[slot_at],
            device_id=side_id(peer),
            device_id_type=MESH,
        )

    @pl.loop(1, blk_count)
    def _(step):
        line_copy(line_peer(step), blk).start()

    @pl.loop(1, blk_count)
    def _(step):
        data_copy(line_peer(step), blk).start()

    fields, levels, columns = tracers.shape
    for small in small_copies[3:]:
        small.wait()
    depth = depth_ref[...]
    level_at = lax.broadcasted_iota(jnp.int32, (levels, columns), 0)
    wet = jnp.where(level_at < depth, 1.0, 0.0)
    couple[0:1, :] = jnp.zeros((1, columns), jnp.float32)
    couple[1:levels, :] = diffusivity_ref[...] * wet[1:levels]
    couple[levels : levels + 1, :] = jnp.zeros((1, columns), jnp.float32)
    tracers_copy.wait()

    @pl.loop(0, fields)
    def _(f):
        at = pl.ds(pl.multiple_of(f * levels, levels), levels)
        for o in range(ocean_blocks):
            lanes = slice(o * width, (o + 1) * width)
            given[o, at, :] = tracers[f, :, lanes].astype(jnp.float32)

    def level_rows(k):
        return pl.ds(k, fields, stride=levels)

    def put_level(k, held):
        for o in range(ocean_blocks):
            mixed_ref[o, level_rows(k), :] = held[:, o * width : (o + 1) * width]

    def first_level(k, held):
        state_row, unit, previous = held
        at = pl.ds(k, 1)
        below, above = couple[at, :], couple[pl.ds(k + 1, 1), :]
        inverse = 1.0 / (1.0 + below + above - below * previous)
        previous = above * inverse
        kept = jnp.where(depth > k, inverse, 0.0)
        passed = below * inverse
        weight[at, :], carry[at, :], ratio[at, :] = kept, passed, previous
        read = [given[o, level_rows(k), :] for o in range(ocean_blocks)]
        state_row = jnp.concatenate(read, axis=1) * kept + passed * state_row
        state[k] = state_row
        unit = jnp.where(k == 0, kept, 0.0) + passed * unit
        response_ref[0, at, :] = unit
        return state_row, unit, previous

    def forward_level(k, held):
        state_row, unit = held
        at = pl.ds(k, 1)
        kept, passed = weight[at, :], carry[at, :]
        state_row = state[k] * kept + passed * state_row
        state[k] = state_row
        unit = response_ref[0, at, :] * kept + passed * unit
        response_ref[1, at, :] = unit
        return state_row, unit

    def back_level(k, held):
        state_row, unit = held
        at = pl.ds(k, 1)
        share = ratio[at, :]
        state_row = state[k] + share * state_row
        state[k] = state_row
        unit = response_ref[0, at, :] + share * unit
        response_ref[0, at, :] = unit
        return state_row, unit

    def last_level(k, held):
        state_row, unit = held
        at = pl.ds(k, 1)
        share = ratio[at, :]
        state_row = state[k] + share * state_row
        put_level(k, state_row)
        unit = response_ref[1, at, :] + share * unit
        response_ref[1, at, :] = unit
        return state_row, unit

    def go_back(level, held):
        held = level(levels - 2, held)
        unroll = 5 if (levels - 2) % 5 == 0 else 1
        lax.fori_loop(0, levels - 2, lambda i, h: level(levels - 3 - i, h), held, unroll=unroll)

    no_row = jnp.zeros((1, columns), jnp.float32)
    nothing = jnp.zeros((fields, columns), jnp.float32)
    bottom = lax.fori_loop(0, levels, first_level, (nothing, no_row, no_row), unroll=4)[:2]

    @pl.loop(1, blk_count)
    def _(step):
        peer = line_peer(step)
        line_copy(peer, peer).wait_recv()

    summed = line_totals[0]
    for p in range(1, blk_count):
        summed = summed + line_totals[p]
    line_sum[...] = summed

    @pl.loop(1, side_count)
    def _(step):
        side_copy(side_peer(step), side).start()

    go_back(back_level, bottom)
    bottom = lax.fori_loop(0, levels, forward_level, (nothing, no_row), unroll=4)
    put_level(levels - 1, bottom[0])
    go_back(last_level, bottom)

    @pl.loop(1, side_count)
    def _(step):
        peer = side_peer(step)
        side_copy(peer, peer).wait_recv()

    side_totals[side] = line_sum[...]
    everything = side_totals[0]
    for p in range(1, side_count):
        everything = everything + side_totals[p]
    correction = jnp.transpose(jnp.broadcast_to(everything[0:1, :] * inverse_columns, (rows, rows)))

    @pl.loop(1, blk_count)
    def _(step):
        peer = line_peer(step)
        data_copy(peer, peer).wait_recv()

    arrived[blk] = outgoing[blk]
    for o in range(ocean_blocks):
        lanes = slice(o * width, (o + 1) * width)
        forced = arrived[0, :, lanes].astype(jnp.float32)
        for p in range(1, blk_count):
            forced = forced + arrived[p, :, lanes].astype(jnp.float32)
        forced_rows[o] = forced + correction
        for s in range(subs):
            forced_ref[s, :, lanes] = forced_rows[o, pl.ds(s, fields, stride=subs), :]

    @pl.loop(1, blk_count)
    def _(step):
        peer = line_peer(step)
        line_copy(peer, blk).wait_send()
        data_copy(peer, blk).wait_send()

    @pl.loop(1, side_count)
    def _(step):
        side_copy(side_peer(step), side).wait_send()


def join_kernel(parts, mixed_ref, response_ref, forced_ref, result_hbm, result, sems):
    fields, levels, columns = result.shape
    halves, _, width = mixed_ref.shape
    near, far = response_ref[0], response_ref[1]
    part = fields // parts

    def copy(n):
        at = pl.ds(n * part, part)
        return pltpu.make_async_copy(result.at[at], result_hbm.at[at], sems.at[n])

    for n in range(parts):
        for f in range(n * part, (n + 1) * part):
            at = slice(f * levels, (f + 1) * levels)
            mixed = jnp.concatenate([mixed_ref[o, at, :] for o in range(halves)], axis=1)
            early = forced_ref[0, f : f + 1, :]
            late = forced_ref[1, f : f + 1, :]
            result[f] = mixed + far * early + near * late
        copy(n).start()
    for n in range(parts):
        copy(n).wait()


def body(
    atm_flux,
    tile_bank,
    pair_count,
    pair_source,
    pair_tile,
    pair_target,
    tracers,
    diffusivity,
    column_depth,
):
    subs, fields, atm_rows = atm_flux.shape
    width = tile_bank.shape[1]
    block_count = atm_rows // width
    levels, _, columns = tracers.shape
    ocean_blocks = columns // width
    blk_count, grp_count = lax.axis_size("blk"), lax.axis_size("grp")
    side_count = lax.axis_size("sec") * grp_count
    pairs = pair_source.shape[0]
    rows = up(subs * fields, 128)
    slot_count = up(pairs + blk_count * ocean_blocks, 2)
    steps = slot_count // 2
    steps_up = up(steps, 4)
    slots = up(2 * steps_up, 128)
    f32, bf16 = jnp.float32, jnp.bfloat16
    vmem = pl.BlockSpec(memory_space=pltpu.VMEM)
    anywhere = pl.BlockSpec(memory_space=pl.ANY)
    mixed, response, forced = pl.pallas_call(
        functools.partial(
            couple_kernel,
            blk_count,
            grp_count,
            side_count,
            ocean_blocks,
            ocean_blocks / block_count,
            1.0 / (columns * blk_count * side_count),
        ),
        out_shape=(
            jax.ShapeDtypeStruct((ocean_blocks, fields * levels, width), f32),
            jax.ShapeDtypeStruct((2, levels, columns), f32),
            jax.ShapeDtypeStruct((subs, fields, columns), f32),
        ),
        in_specs=[pl.BlockSpec(memory_space=pltpu.SMEM)]
        + [pl.BlockSpec(memory_space=pltpu.HBM)] * 8,
        out_specs=(vmem, vmem, vmem),
        scratch_shapes=[
            pltpu.VMEM((1, pairs), jnp.int32),
            pltpu.VMEM((1, pairs), jnp.int32),
            pltpu.VMEM((1, pairs), jnp.int32),
            pltpu.VMEM((levels - 1, columns), f32),
            pltpu.VMEM((1, columns), jnp.int32),
            pltpu.VMEM((fields, subs, atm_rows), bf16),
            pltpu.VMEM(tile_bank.shape, bf16),
            pltpu.VMEM((fields, levels, columns), bf16),
            pltpu.VMEM((ocean_blocks, fields * levels, width), f32),
            pltpu.VMEM((levels, fields, columns), f32),
            pltpu.VMEM((ocean_blocks, rows, width), f32),
            pltpu.VMEM((block_count + 1, rows, width), bf16),
            pltpu.VMEM((steps_up + 1, rows, width), f32),
            pltpu.VMEM((16, slots), jnp.int32),
            pltpu.SMEM((16, slots), jnp.int32),
            pltpu.VMEM((blk_count, rows, columns), bf16),
            pltpu.VMEM((blk_count, rows, columns), bf16),
            pltpu.VMEM((rows, width), f32),
            pltpu.VMEM((blk_count, 8, rows), f32),
            pltpu.VMEM((8, rows), f32),
            pltpu.VMEM((side_count, 8, rows), f32),
            pltpu.VMEM((levels + 8, columns), f32),
            pltpu.VMEM((levels, columns), f32),
            pltpu.VMEM((levels, columns), f32),
            pltpu.VMEM((levels, columns), f32),
            pltpu.SemaphoreType.DMA((9,)),
            pltpu.SemaphoreType.DMA((blk_count,)),
            pltpu.SemaphoreType.DMA((blk_count,)),
            pltpu.SemaphoreType.DMA((blk_count,)),
            pltpu.SemaphoreType.DMA((blk_count,)),
            pltpu.SemaphoreType.DMA((side_count,)),
            pltpu.SemaphoreType.DMA((side_count,)),
        ],
        compiler_params=pltpu.CompilerParams(
            collective_id=0, has_side_effects=True, vmem_limit_bytes=48 * 1024 * 1024
        ),
    )(
        pair_count,
        *[
            pltpu.with_memory_space_constraint(operand, pltpu.HBM)
            for operand in (
                pair_source.reshape(1, pairs),
                pair_tile.reshape(1, pairs),
                pair_target.reshape(1, pairs),
                diffusivity,
                column_depth.reshape(1, columns),
                jnp.transpose(atm_flux, (1, 0, 2)),
                tile_bank,
                jnp.transpose(tracers, (1, 0, 2)),
            )
        ]
    )
    parts = 10 if fields % 10 == 0 else 1
    result = pl.pallas_call(
        functools.partial(join_kernel, parts),
        out_shape=jax.ShapeDtypeStruct((fields, levels, columns), f32),
        in_specs=[vmem, vmem, vmem],
        out_specs=anywhere,
        scratch_shapes=[
            pltpu.VMEM((fields, levels, columns), f32),
            pltpu.SemaphoreType.DMA((parts,)),
        ],
        compiler_params=pltpu.CompilerParams(vmem_limit_bytes=16 * 1024 * 1024),
    )(mixed, response, forced)
    return jnp.transpose(result, (1, 0, 2))


def solution(mesh):
    over = ("sec", "grp", "blk")
    placed = (
        P(None, None, over),
        P(),
        P(over),
        P(over),
        P(over),
        P(over),
        P(None, None, over),
        P(None, over),
        P(over),
    )
    return jax.shard_map(
        body, mesh=mesh, in_specs=placed, out_specs=P(None, None, over), check_vma=False
    )
```

```python
import functools

import jax
import jax.numpy as jnp
from jax import lax
from jax.experimental import pallas as pl
from jax.experimental.pallas import tpu as pltpu
from jax.sharding import PartitionSpec as P

MESH = pl.DeviceIdType.MESH


def up(value, unit):
    return -(-value // unit) * unit


def couple_kernel(
    blk_count,
    grp_count,
    side_count,
    ocean_blocks,
    scale,
    inverse_columns,
    count_ref,
    source_hbm,
    tile_hbm,
    target_hbm,
    diffusivity_hbm,
    depth_hbm,
    flux_hbm,
    bank_hbm,
    tracers_hbm,
    mixed_ref,
    response_ref,
    forced_ref,
    source_ref,
    tile_ref,
    target_ref,
    diffusivity_ref,
    depth_ref,
    flux,
    bank,
    tracers,
    given,
    state,
    forced_rows,
    blocks,
    running,
    lists,
    lists_smem,
    outgoing,
    arrived,
    own_total,
    line_totals,
    line_sum,
    side_totals,
    couple,
    weight,
    carry,
    ratio,
    local_sem,
    bank_sem,
    send_sem,
    recv_sem,
    line_send,
    line_recv,
    side_send,
    side_recv,
):
    sec, grp, blk = lax.axis_index("sec"), lax.axis_index("grp"), lax.axis_index("blk")
    side = sec * grp_count + grp

    def line_peer(step):
        return lax.rem(blk + step, blk_count)

    def side_peer(step):
        return lax.rem(side + step, side_count)

    def line_id(peer):
        return (sec, grp, peer)

    def side_id(peer):
        return (peer // grp_count, lax.rem(peer, grp_count), blk)

    small_copies = [
        pltpu.make_async_copy(given_hbm, ref, local_sem.at[4 + i])
        for i, (given_hbm, ref) in enumerate(
            (
                (target_hbm, target_ref),
                (source_hbm, source_ref),
                (tile_hbm, tile_ref),
                (depth_hbm, depth_ref),
                (diffusivity_hbm, diffusivity_ref),
            )
        )
    ]
    for small in small_copies[:3]:
        small.start()
    flux_copy = pltpu.make_async_copy(flux_hbm, flux, local_sem.at[0])
    bank_part = bank.shape[0] // bank_sem.shape[0]
    bank_copies = [
        pltpu.make_async_copy(
            bank_hbm.at[pl.ds(n * bank_part, bank_part)],
            bank.at[pl.ds(n * bank_part, bank_part)],
            bank_sem.at[n],
        )
        for n in range(bank_sem.shape[0])
    ]
    tracers_copy = pltpu.make_async_copy(tracers_hbm, tracers, local_sem.at[2])
    flux_copy.start()
    for part in bank_copies:
        part.start()
    for small in small_copies[3:]:
        small.start()
    tracers_copy.start()

    barrier = pltpu.get_barrier_semaphore()

    @pl.loop(1, blk_count)
    def _(step):
        pl.semaphore_signal(barrier, inc=1, device_id=line_id(line_peer(step)), device_id_type=MESH)

    @pl.loop(1, side_count)
    def _(step):
        pl.semaphore_signal(barrier, inc=1, device_id=side_id(side_peer(step)), device_id_type=MESH)

    pairs = source_ref.shape[1]
    slots = lists.shape[1]
    for small in small_copies[:3]:
        small.wait()
    live_count = count_ref[0]
    square = (pairs, pairs)
    row_at = lax.broadcasted_iota(jnp.int32, square, 0)
    lane_at = lax.broadcasted_iota(jnp.int32, square, 1)
    target_row = jnp.broadcast_to(target_ref[...], square)
    target_col = jnp.transpose(target_row)
    source_col = jnp.transpose(jnp.broadcast_to(source_ref[...], square))
    tile_col = jnp.transpose(jnp.broadcast_to(tile_ref[...], square))
    live_row = lane_at < live_count
    live_col = row_at < live_count
    hits = jnp.where((target_col == lane_at) & live_col, 1, 0)
    counts = jnp.sum(hits, axis=0, keepdims=True)
    padded = jnp.broadcast_to(lax.div(counts + 1, 2) * 2, square)
    before = jnp.where(lane_at < target_col, padded, 0)
    rank = jnp.where((target_row == target_col) & (lane_at < row_at) & live_row, 1, 0)
    slot = jnp.sum(before + rank, axis=1, keepdims=True)
    slot = jnp.where(live_col, jnp.broadcast_to(slot, square), slots)
    block_count = blocks.shape[0] - 1
    steps = running.shape[0] - 1
    lists[...] = jnp.zeros(lists.shape, jnp.int32)
    for first in range(0, slots, pairs):
        lanes = slice(first, first + pairs)
        chosen = slot == lane_at + first
        sources = jnp.sum(jnp.where(chosen, source_col - block_count, 0), axis=0, keepdims=True)
        tiles = jnp.sum(jnp.where(chosen, tile_col, 0), axis=0, keepdims=True)
        targets = jnp.sum(jnp.where(chosen, target_col + 1, 0), axis=0, keepdims=True)
        lists[0:1, lanes] = jnp.clip(sources + block_count, 0, block_count)
        lists[1:2, lanes] = jnp.clip(tiles, 0, bank.shape[0] - 1)
        lists[2:3, lanes] = targets
    upto = jnp.where(row_at <= lane_at, jnp.transpose(padded), 0)
    ends = lax.div(jnp.sum(upto, axis=0, keepdims=True), 2) - 1
    lists[8:9, 0:pairs] = jnp.where(counts > 0, jnp.clip(ends, 0, steps), steps)
    lists_copy = pltpu.make_async_copy(lists, lists_smem, local_sem.at[3])
    lists_copy.start()

    flux_copy.wait()
    fields, subs = flux.shape[0], flux.shape[1]
    rows, width = blocks.shape[1], blocks.shape[2]
    stack = fields * subs
    blocks[...] = jnp.zeros(blocks.shape, blocks.dtype)
    for b in range(block_count):
        blocks[b, 0:stack, :] = flux[:, :, b * width : (b + 1) * width].reshape(stack, width)
    running[steps] = jnp.zeros((rows, width), jnp.float32)
    spread = jnp.zeros((rows, width), jnp.float32)
    for b in range(block_count):
        spread = spread + blocks[b].astype(jnp.float32)
    own_total[...] = spread * scale

    lists_copy.wait()
    for part in bank_copies:
        part.wait()

    def add_step(step, held):
        total, last = held
        first, second = 2 * step, 2 * step + 1
        target = lists_smem[2, first]
        left = jnp.concatenate([blocks[lists_smem[0, first]], blocks[lists_smem[0, second]]], axis=1)
        right = jnp.concatenate([bank[lists_smem[1, first]], bank[lists_smem[1, second]]], axis=0)
        keep = jnp.where(target == last, 1.0, 0.0).astype(jnp.float32)
        total = total * keep + jnp.dot(left, right, preferred_element_type=jnp.float32)
        running[step] = total
        return total, target

    lax.fori_loop(
        0, steps, add_step, (jnp.zeros((rows, width), jnp.float32), jnp.int32(-1)), unroll=steps // 2
    )

    @pl.loop(0, blk_count)
    def _(peer):
        spread = own_total[...]
        for o in range(ocean_blocks):
            out = running[lists_smem[8, peer * ocean_blocks + o]].astype(jnp.bfloat16)
            outgoing[peer, :, o * width : (o + 1) * width] = out
            spread = spread - out.astype(jnp.float32)
        own_total[...] = spread

    total_row = jnp.sum(jnp.transpose(own_total[...]), axis=0, keepdims=True)
    line_totals[blk] = jnp.broadcast_to(total_row, (8, rows))

    pl.semaphore_wait(barrier, blk_count - 1 + side_count - 1)

    def line_copy(peer, slot_at):
        return pltpu.make_async_remote_copy(
            src_ref=line_totals.at[blk],
            dst_ref=line_totals.at[slot_at],
            send_sem=line_send.at[peer],
            recv_sem=line_recv.at[slot_at],
            device_id=line_id(peer),
            device_id_type=MESH,
        )

    def data_copy(peer, slot_at):
        return pltpu.make_async_remote_copy(
            src_ref=outgoing.at[peer],
            dst_ref=arrived.at[slot_at],
            send_sem=send_sem.at[peer],
            recv_sem=recv_sem.at[slot_at],
            device_id=line_id(peer),
            device_id_type=MESH,
        )

    def side_copy(peer, slot_at):
        return pltpu.make_async_remote_copy(
            src_ref=line_sum,
            dst_ref=side_totals.at[slot_at],
            send_sem=side_send.at[peer],
            recv_sem=side_recv.at[slot_at],
            device_id=side_id(peer),
            device_id_type=MESH,
        )

    @pl.loop(1, blk_count)
    def _(step):
        line_copy(line_peer(step), blk).start()

    @pl.loop(1, blk_count)
    def _(step):
        distance = blk_count - step

        @pl.when(blk + distance < blk_count)
        def _():
            data_copy(blk + distance, blk).start()

        @pl.when(blk >= distance)
        def _():
            data_copy(blk - distance, blk).start()

    fields, levels, columns = tracers.shape
    for small in small_copies[3:]:
        small.wait()
    depth = depth_ref[...]
    level_at = lax.broadcasted_iota(jnp.int32, (levels, columns), 0)
    wet = jnp.where(level_at < depth, 1.0, 0.0)
    couple[0:1, :] = jnp.zeros((1, columns), jnp.float32)
    couple[1:levels, :] = diffusivity_ref[...] * wet[1:levels]
    couple[levels : levels + 1, :] = jnp.zeros((1, columns), jnp.float32)
    tracers_copy.wait()

    @pl.loop(0, fields)
    def _(f):
        at = pl.ds(pl.multiple_of(f * levels, levels), levels)
        for o in range(ocean_blocks):
            lanes = slice(o * width, (o + 1) * width)
            given[o, at, :] = tracers[f, :, lanes].astype(jnp.float32)

    def level_rows(k):
        return pl.ds(k, fields, stride=levels)

    def put_level(k, held):
        for o in range(ocean_blocks):
            mixed_ref[o, level_rows(k), :] = held[:, o * width : (o + 1) * width]

    def first_level(k, held):
        state_row, unit, previous = held
        at = pl.ds(k, 1)
        below, above = couple[at, :], couple[pl.ds(k + 1, 1), :]
        inverse = 1.0 / (1.0 + below + above - below * previous)
        previous = above * inverse
        kept = jnp.where(depth > k, inverse, 0.0)
        passed = below * inverse
        weight[at, :], carry[at, :], ratio[at, :] = kept, passed, previous
        read = [given[o, level_rows(k), :] for o in range(ocean_blocks)]
        state_row = jnp.concatenate(read, axis=1) * kept + passed * state_row
        state[k] = state_row
        unit = jnp.where(k == 0, kept, 0.0) + passed * unit
        response_ref[0, at, :] = unit
        return state_row, unit, previous

    def forward_level(k, held):
        state_row, unit = held
        at = pl.ds(k, 1)
        kept, passed = weight[at, :], carry[at, :]
        state_row = state[k] * kept + passed * state_row
        state[k] = state_row
        unit = response_ref[0, at, :] * kept + passed * unit
        response_ref[1, at, :] = unit
        return state_row, unit

    def back_level(k, held):
        state_row, unit = held
        at = pl.ds(k, 1)
        share = ratio[at, :]
        state_row = state[k] + share * state_row
        state[k] = state_row
        unit = response_ref[0, at, :] + share * unit
        response_ref[0, at, :] = unit
        return state_row, unit

    def last_level(k, held):
        state_row, unit = held
        at = pl.ds(k, 1)
        share = ratio[at, :]
        state_row = state[k] + share * state_row
        put_level(k, state_row)
        unit = response_ref[1, at, :] + share * unit
        response_ref[1, at, :] = unit
        return state_row, unit

    def go_back(level, held):
        held = level(levels - 2, held)
        unroll = 5 if (levels - 2) % 5 == 0 else 1
        lax.fori_loop(0, levels - 2, lambda i, h: level(levels - 3 - i, h), held, unroll=unroll)

    no_row = jnp.zeros((1, columns), jnp.float32)
    nothing = jnp.zeros((fields, columns), jnp.float32)
    bottom = lax.fori_loop(0, levels, first_level, (nothing, no_row, no_row), unroll=4)[:2]

    @pl.loop(1, blk_count)
    def _(step):
        peer = line_peer(step)
        line_copy(peer, peer).wait_recv()

    summed = line_totals[0]
    for p in range(1, blk_count):
        summed = summed + line_totals[p]
    line_sum[...] = summed

    @pl.loop(1, side_count)
    def _(step):
        side_copy(side_peer(step), side).start()

    go_back(back_level, bottom)
    bottom = lax.fori_loop(0, levels, forward_level, (nothing, no_row), unroll=4)
    put_level(levels - 1, bottom[0])
    go_back(last_level, bottom)

    @pl.loop(1, side_count)
    def _(step):
        peer = side_peer(step)
        side_copy(peer, peer).wait_recv()

    side_totals[side] = line_sum[...]
    everything = side_totals[0]
    for p in range(1, side_count):
        everything = everything + side_totals[p]
    correction = jnp.transpose(jnp.broadcast_to(everything[0:1, :] * inverse_columns, (rows, rows)))

    @pl.loop(1, blk_count)
    def _(step):
        peer = line_peer(step)
        data_copy(peer, peer).wait_recv()

    arrived[blk] = outgoing[blk]
    for o in range(ocean_blocks):
        lanes = slice(o * width, (o + 1) * width)
        forced = arrived[0, :, lanes].astype(jnp.float32)
        for p in range(1, blk_count):
            forced = forced + arrived[p, :, lanes].astype(jnp.float32)
        forced_rows[o] = forced + correction
        for s in range(subs):
            forced_ref[s, :, lanes] = forced_rows[o, pl.ds(s, fields, stride=subs), :]

    @pl.loop(1, blk_count)
    def _(step):
        peer = line_peer(step)
        line_copy(peer, blk).wait_send()
        data_copy(peer, blk).wait_send()

    @pl.loop(1, side_count)
    def _(step):
        side_copy(side_peer(step), side).wait_send()


def join_kernel(parts, mixed_ref, response_ref, forced_ref, result_hbm, result, sems):
    fields, levels, columns = result.shape
    halves, _, width = mixed_ref.shape
    near, far = response_ref[0], response_ref[1]
    part = fields // parts

    def copy(n):
        at = pl.ds(n * part, part)
        return pltpu.make_async_copy(result.at[at], result_hbm.at[at], sems.at[n])

    for n in range(parts):
        for f in range(n * part, (n + 1) * part):
            at = slice(f * levels, (f + 1) * levels)
            mixed = jnp.concatenate([mixed_ref[o, at, :] for o in range(halves)], axis=1)
            early = forced_ref[0, f : f + 1, :]
            late = forced_ref[1, f : f + 1, :]
            result[f] = mixed + far * early + near * late
        copy(n).start()
    for n in range(parts):
        copy(n).wait()


def body(
    atm_flux,
    tile_bank,
    pair_count,
    pair_source,
    pair_tile,
    pair_target,
    tracers,
    diffusivity,
    column_depth,
):
    subs, fields, atm_rows = atm_flux.shape
    width = tile_bank.shape[1]
    block_count = atm_rows // width
    levels, _, columns = tracers.shape
    ocean_blocks = columns // width
    blk_count, grp_count = lax.axis_size("blk"), lax.axis_size("grp")
    side_count = lax.axis_size("sec") * grp_count
    pairs = pair_source.shape[0]
    rows = up(subs * fields, 128)
    slot_count = up(pairs + blk_count * ocean_blocks, 2)
    steps = slot_count // 2
    steps_up = up(steps, 4)
    slots = up(2 * steps_up, 128)
    f32, bf16 = jnp.float32, jnp.bfloat16
    vmem = pl.BlockSpec(memory_space=pltpu.VMEM)
    anywhere = pl.BlockSpec(memory_space=pl.ANY)
    mixed, response, forced = pl.pallas_call(
        functools.partial(
            couple_kernel,
            blk_count,
            grp_count,
            side_count,
            ocean_blocks,
            ocean_blocks / block_count,
            1.0 / (columns * blk_count * side_count),
        ),
        out_shape=(
            jax.ShapeDtypeStruct((ocean_blocks, fields * levels, width), f32),
            jax.ShapeDtypeStruct((2, levels, columns), f32),
            jax.ShapeDtypeStruct((subs, fields, columns), f32),
        ),
        in_specs=[pl.BlockSpec(memory_space=pltpu.SMEM)]
        + [pl.BlockSpec(memory_space=pltpu.HBM)] * 8,
        out_specs=(vmem, vmem, vmem),
        scratch_shapes=[
            pltpu.VMEM((1, pairs), jnp.int32),
            pltpu.VMEM((1, pairs), jnp.int32),
            pltpu.VMEM((1, pairs), jnp.int32),
            pltpu.VMEM((levels - 1, columns), f32),
            pltpu.VMEM((1, columns), jnp.int32),
            pltpu.VMEM((fields, subs, atm_rows), bf16),
            pltpu.VMEM(tile_bank.shape, bf16),
            pltpu.VMEM((fields, levels, columns), bf16),
            pltpu.VMEM((ocean_blocks, fields * levels, width), f32),
            pltpu.VMEM((levels, fields, columns), f32),
            pltpu.VMEM((ocean_blocks, rows, width), f32),
            pltpu.VMEM((block_count + 1, rows, width), bf16),
            pltpu.VMEM((steps_up + 1, rows, width), f32),
            pltpu.VMEM((16, slots), jnp.int32),
            pltpu.SMEM((16, slots), jnp.int32),
            pltpu.VMEM((blk_count, rows, columns), bf16),
            pltpu.VMEM((blk_count, rows, columns), bf16),
            pltpu.VMEM((rows, width), f32),
            pltpu.VMEM((blk_count, 8, rows), f32),
            pltpu.VMEM((8, rows), f32),
            pltpu.VMEM((side_count, 8, rows), f32),
            pltpu.VMEM((levels + 8, columns), f32),
            pltpu.VMEM((levels, columns), f32),
            pltpu.VMEM((levels, columns), f32),
            pltpu.VMEM((levels, columns), f32),
            pltpu.SemaphoreType.DMA((9,)),
            pltpu.SemaphoreType.DMA((8 if tile_bank.shape[0] % 8 == 0 else 1,)),
            pltpu.SemaphoreType.DMA((blk_count,)),
            pltpu.SemaphoreType.DMA((blk_count,)),
            pltpu.SemaphoreType.DMA((blk_count,)),
            pltpu.SemaphoreType.DMA((blk_count,)),
            pltpu.SemaphoreType.DMA((side_count,)),
            pltpu.SemaphoreType.DMA((side_count,)),
        ],
        compiler_params=pltpu.CompilerParams(
            collective_id=0, has_side_effects=True, vmem_limit_bytes=48 * 1024 * 1024
        ),
    )(
        pair_count,
        *[
            pltpu.with_memory_space_constraint(operand, pltpu.HBM)
            for operand in (
                pair_source.reshape(1, pairs),
                pair_tile.reshape(1, pairs),
                pair_target.reshape(1, pairs),
                diffusivity,
                column_depth.reshape(1, columns),
                jnp.transpose(atm_flux, (1, 0, 2)),
                tile_bank,
                jnp.transpose(tracers, (1, 0, 2)),
            )
        ]
    )
    parts = 10 if fields % 10 == 0 else 1
    result = pl.pallas_call(
        functools.partial(join_kernel, parts),
        out_shape=jax.ShapeDtypeStruct((fields, levels, columns), f32),
        in_specs=[vmem, vmem, vmem],
        out_specs=anywhere,
        scratch_shapes=[
            pltpu.VMEM((fields, levels, columns), f32),
            pltpu.SemaphoreType.DMA((parts,)),
        ],
        compiler_params=pltpu.CompilerParams(vmem_limit_bytes=16 * 1024 * 1024),
    )(mixed, response, forced)
    return jnp.transpose(result, (1, 0, 2))


def solution(mesh):
    over = ("sec", "grp", "blk")
    placed = (
        P(None, None, over),
        P(),
        P(over),
        P(over),
        P(over),
        P(over),
        P(None, None, over),
        P(None, over),
        P(over),
    )
    return jax.shard_map(
        body, mesh=mesh, in_specs=placed, out_specs=P(None, None, over), check_vma=False
    )
```
